256 devices in a mesh: wave: 64 (over x, z, core), lev: 4 (over y).
Axes of the slice: x: 4, y: 4, z: 8, core: 2. Of those that a mesh axis runs over, the one named last changes fastest.
Arguments:
- spectral: bfloat16 [1280, 3, 2, 24, 1280], P('wave', None, None, 'lev'), may hold values from -0.119628906 to 0.119628906
- legendre: bfloat16 [1280, 1280, 512], P(('wave', 'lev')), may hold values from -0.15625 to 0.15625
- wave_map: int32 [1280], replicated, may hold values from 0 to 1279, each once
- row_map: int32 [512], replicated, may hold values from 0 to 511, each once
- points: int32 [512], replicated, may hold values from 20 to 5136, as said below
- row_weight: float32 [512], replicated, may hold values from 40 to 400
- thickness: float32 [24], replicated, may hold values from 0.3 to 3
Outputs:
- spec_tend: bfloat16 [1280, 3, 2, 24, 1280], P('wave', None, None, 'lev')
- grid_tend: bfloat16 [512, 24, 5376], P(('wave', 'lev'))
The draws below stay inside these ranges and needn't reach their ends.
Inputs may be any that keep to these rules, and one draw needn't show every extreme that they name: `wave_map`: each slot holds a different wavenumber. `row_map`: each latitude row is held by one slot. The rows are distinct rows of an octahedral grid of 2560 rows; a row j rows from the nearer pole (j from 0) has 20 + 4 j points; one row lies next to the equator.
All inputs are finite; a program needn't handle non-finite values.
Results may differ from the reference program's by a relative error of at most 0.009.
Values may be sent and summed in bfloat16 or wider, within the bound.
A program may use at most 64 MiB of HBM per device.

```python
import math
import jax
import jax.numpy as jnp
from jax import lax

M = 1280
LEV = 24
ROWS = 512
PBUF = 5376


def draw_points(key, part):
    key = jax.random.fold_in(key, 11)
    chosen = jax.random.permutation(key, 2 * M)[:ROWS].astype(jnp.int32)
    has_middle = jnp.any(chosen == M - 1)
    chosen = jnp.where(has_middle, chosen, chosen.at[0].set(M - 1))
    from_pole = jnp.minimum(chosen, 2 * M - 1 - chosen)
    return (20 + 4 * from_pole).astype(jnp.int32)


def shard_levels(stream_key, shape, shards, smallest, top_value):
    def one(position, parts):
        heights = jax.random.uniform(jax.random.fold_in(jax.random.fold_in(stream_key, 6), position), (parts,), jnp.float32, smallest / len(shards), top_value / len(shards))
        return jnp.repeat(jnp.exp(heights), shape[position] // parts).reshape((-1,) + (1,) * (len(shape) - position - 1))

    level = one(*shards[0])
    for cut in shards[1:]:
        level = level * one(*cut)
    return level


def gaussian(own_key, extent, deviation, limit, shards=(), kind=jnp.bfloat16):
    level = shard_levels(own_key, extent, shards, -0.22, 0.18) if shards else 1.0
    result = jax.random.normal(own_key, extent, jnp.float32) * deviation * level
    return jnp.minimum(jnp.maximum(result, -limit), limit).astype(kind)


def setup_inputs(seed: int = 0) -> dict:
    streams_of = jax.random.split(jax.random.key(seed), 8)
    spectral = gaussian(streams_of[0], (M, 3, 2, LEV, M), 0.02, 0.119628906, ((0, 64), (3, 4)))
    legendre = gaussian(streams_of[1], (M, M, ROWS), M ** -0.5, 0.15625, ((0, 256),))
    wave_map = jax.random.permutation(streams_of[2], M).astype(jnp.int32)
    row_map = jax.random.permutation(streams_of[3], ROWS).astype(jnp.int32)
    points = draw_points(jax.random.fold_in(streams_of[7], 71), 0)
    row_weight = jnp.clip(jnp.exp(jax.random.uniform(streams_of[5], (ROWS,), jnp.float32, math.log(40.0), math.log(400.0))), 40.0, 400.0)
    thickness = jnp.clip(jnp.exp(jax.random.uniform(streams_of[6], (LEV,), jnp.float32, math.log(0.3), math.log(3.0))), 0.3, 3.0)
    return {"spectral": spectral, "legendre": legendre, "wave_map": wave_map, "row_map": row_map, "points": points, "row_weight": row_weight, "thickness": thickness}


adiabatic_exponent = 2.0 / 7.0


def row_tables(row_points, slot_waves, first_point, width):
    point_ids = first_point + jnp.arange(width, dtype=jnp.int32)
    residues = (slot_waves[:, None] * point_ids[None, :]) % row_points
    angles = (2.0 * jnp.pi) * residues.astype(jnp.float32) / row_points.astype(jnp.float32)
    active = (2 * slot_waves[:, None] < row_points) & (point_ids[None, :] < row_points)
    cosines = jnp.where(active, jnp.cos(angles), 0.0).astype(jnp.bfloat16)
    sine_part = jnp.where(active, -jnp.sin(angles), 0.0).astype(jnp.bfloat16)
    return jnp.concatenate([cosines, sine_part], axis=0)


def tendencies(quantity_pile, thickness):
    vorticity = quantity_pile[0]
    flow_spreading_grid = quantity_pile[1]
    thermal_state_grid = quantity_pile[2]
    upward_motion = -jnp.cumsum(thickness[:, None] * flow_spreading_grid, axis=0)
    ground_barometric_load = jnp.cumsum(thickness) - 0.5 * thickness
    rotation_rate_change = -vorticity * flow_spreading_grid
    spreading_rate_change = 0.5 * (vorticity * vorticity - flow_spreading_grid * flow_spreading_grid)
    warming_rate = -thermal_state_grid * flow_spreading_grid + adiabatic_exponent * thermal_state_grid * upward_motion / ground_barometric_load[:, None]
    return jnp.stack([rotation_rate_change, spreading_rate_change, warming_rate]).astype(jnp.bfloat16)


def row_trip(fourier_row, slot_waves, row_points, row_scale, thickness):
    levels = thickness.shape[0]
    weights = jnp.where(slot_waves == 0, 1.0, 2.0).astype(jnp.float32)
    lifted = (fourier_row.astype(jnp.float32) * weights[:, None, None, None]).astype(jnp.bfloat16)
    left_side = lifted.transpose(1, 3, 2, 0).reshape(3 * levels, 2 * M)
    tables = row_tables(row_points, slot_waves, jnp.int32(0), PBUF).astype(jnp.float32)
    quantity_pile = jnp.dot(left_side.astype(jnp.float32), tables, precision=lax.Precision.HIGHEST)
    tendency = tendencies(quantity_pile.reshape(3, levels, PBUF), thickness)
    direct_sums = jnp.dot(tendency.reshape(3 * levels, PBUF).astype(jnp.float32), tables.T, precision=lax.Precision.HIGHEST)
    back_row = (direct_sums * row_scale).astype(jnp.bfloat16).reshape(3, levels, 2, M).transpose(3, 0, 2, 1)
    return back_row, tendency[2]


def reference(spectral, legendre, wave_map, row_map, points, row_weight, thickness):
    levels = thickness.shape[0]
    kept_mask = jnp.arange(M, dtype=jnp.int32)[None, :] < (M - wave_map)[:, None]
    masked_coefs = jnp.where(kept_mask[:, None, None, None, :], spectral, jnp.zeros((), jnp.bfloat16))

    def inverse_slot(slot_pair):
        slot_coefs, slot_table = slot_pair
        return jnp.dot(slot_coefs.reshape(6 * levels, M).astype(jnp.float32), slot_table.astype(jnp.float32), precision=lax.Precision.HIGHEST).astype(jnp.bfloat16)

    fourier = lax.map(inverse_slot, (masked_coefs, legendre))
    by_row = fourier.reshape(M, 3, 2, levels, ROWS).transpose(4, 0, 1, 2, 3)
    scales = row_weight / points.astype(jnp.float32)

    def one_row(bundle):
        fourier_row, row_points, row_scale = bundle
        return row_trip(fourier_row, wave_map, row_points, row_scale, thickness)

    row_backs, row_temps = lax.map(one_row, (by_row, points, scales))
    returned = row_backs.transpose(1, 2, 3, 4, 0).reshape(M, 6 * levels, ROWS)

    def direct_slot(slot_pair):
        slot_back, slot_table = slot_pair
        return jnp.dot(slot_back.astype(jnp.float32), slot_table.astype(jnp.float32).T, precision=lax.Precision.HIGHEST)

    direct_sums = lax.map(direct_slot, (returned, legendre))
    spec_tend = jnp.where(kept_mask[:, None, :], direct_sums, 0.0).astype(jnp.bfloat16).reshape(M, 3, 2, levels, M)
    grid_tend = row_temps[row_map]
    return spec_tend, grid_tend
```

```python
import functools

import jax
import jax.numpy as jnp
from jax import lax
from jax.experimental import pallas as pl
from jax.experimental.pallas import tpu as pltpu
from jax.sharding import PartitionSpec as P

PBUF = 5376
BLOCK = 768
LANES = 128

adiabatic_exponent = 2.0 / 7.0

cos_terms = (0.9999999857, -19.73920338, 64.9390589, -85.44903786, 60.15837722, -25.93212729, 6.478082977)
sin_terms = (6.283185301, -41.34169993, 81.60510632, -76.70254382, 42.02196627, -14.88466424, 3.21649078)


def turn_cos_sin(turns):
    square = turns * turns
    cosine = jnp.full_like(turns, cos_terms[-1])
    for term in cos_terms[-2::-1]:
        cosine = cosine * square + term
    sine = jnp.full_like(turns, sin_terms[-1])
    for term in sin_terms[-2::-1]:
        sine = sine * square + term
    return cosine, sine * turns


def turns_of(product, count, inverse):
    return (product - count * jnp.round(product * inverse)) * inverse


def table_kernel(points_ref, waves_ref, table_ref):
    row = pl.program_id(0)
    count = points_ref[row].astype(jnp.float32)
    inverse = 1.0 / jnp.full((1, 1), count, jnp.float32)
    waves_all = waves_ref.shape[0]
    chunk = 64

    def one_chunk(index, carry):
        at = pl.multiple_of(index * chunk, chunk)
        waves = waves_ref[pl.ds(at, chunk), :]
        lane = lax.broadcasted_iota(jnp.int32, (chunk, LANES), 1).astype(jnp.float32)
        cosine, sine = turn_cos_sin(turns_of(waves * lane, count, inverse))
        step_cos, step_sin = turn_cos_sin(turns_of(waves * float(LANES), count, inverse))
        for piece in range(BLOCK // LANES):
            where = pl.ds(piece * LANES, LANES)
            table_ref[0, 0, pl.ds(at, chunk), where] = cosine.astype(jnp.bfloat16)
            table_ref[0, 1, pl.ds(at, chunk), where] = (-sine).astype(jnp.bfloat16)
            if piece + 1 < BLOCK // LANES:
                cosine, sine = (
                    cosine * step_cos - sine * step_sin,
                    sine * step_cos + cosine * step_sin,
                )
        return carry

    lax.fori_loop(0, waves_all // chunk, one_chunk, 0)


def make_tables(points, waves):
    rows, waves_all = points.shape[0], waves.shape[0]
    spread = jnp.broadcast_to(waves.astype(jnp.float32)[:, None], (waves_all, LANES))
    return pl.pallas_call(
        table_kernel,
        grid=(rows,),
        out_shape=jax.ShapeDtypeStruct((rows, 2, waves_all, BLOCK), jnp.bfloat16),
        in_specs=[
            pl.BlockSpec(memory_space=pltpu.SMEM),
            pl.BlockSpec((waves_all, LANES), lambda i: (0, 0)),
        ],
        out_specs=pl.BlockSpec((1, 2, waves_all, BLOCK), lambda i: (i, 0, 0, 0)),
        compiler_params=pltpu.CompilerParams(vmem_limit_bytes=40 * 1024 * 1024),
        cost_estimate=pl.CostEstimate(
            flops=rows * waves_all * BLOCK * 40,
            bytes_accessed=rows * waves_all * BLOCK * 4,
            transcendentals=0,
        ),
        name="tables",
    )(points, spread)


def running_sum(values):
    place = lax.broadcasted_iota(jnp.int32, (8, values.shape[1]), 0)
    before = jnp.zeros((1, values.shape[1]), jnp.float32)
    groups = []
    for start in range(0, values.shape[0], 8):
        part = values[start : start + 8]
        for shift in (1, 2, 4):
            part = part + jnp.where(place >= shift, pltpu.roll(part, shift, 0), 0.0)
        part = part + before
        before = part[7:8]
        groups.append(part)
    return jnp.concatenate(groups, axis=0)


def row_kernel(
    points_ref, scale_ref, waves_ref, thick_ref, press_ref, fourier_ref, table_ref,
    back_ref, temp_ref, rotated, grid_part, tend,
):
    row = pl.program_id(0)
    count_int = points_ref[row]
    count = count_int.astype(jnp.float32)
    inverse = 1.0 / jnp.full((1, 1), count, jnp.float32)
    waves = waves_ref[...].astype(jnp.float32)
    waves_all = waves.shape[1]
    fields = fourier_ref.shape[1] // 2
    levels = fields // 3
    blocks = PBUF // BLOCK
    kept = 2.0 * waves < count
    weight = jnp.where(kept, jnp.where(waves == 0.0, 1.0, 2.0), 0.0)
    values = fourier_ref[0].astype(jnp.float32) * weight
    real, imag = values[:fields], values[fields:]

    starts = lax.broadcasted_iota(jnp.int32, (8, waves_all), 0).astype(jnp.float32) * float(BLOCK)
    phase_cos, phase_sin = turn_cos_sin(turns_of(waves * starts, count, inverse))
    for block in range(blocks):
        cosine = phase_cos[block : block + 1]
        sine = phase_sin[block : block + 1]
        there = pl.ds(block * fields, fields)
        rotated[there, :waves_all] = real * cosine - imag * sine
        rotated[there, waves_all:] = real * sine + imag * cosine

    left = rotated[...].astype(jnp.bfloat16)
    for at in range(0, BLOCK, 256):
        right = table_ref[0, :, :, at : at + 256].reshape(2 * waves_all, 256)
        grid_part[:, at : at + 256] = jnp.dot(left, right, preferred_element_type=jnp.float32)

    thick = thick_ref[...]
    factor = adiabatic_exponent / press_ref[...]
    place = lax.broadcasted_iota(jnp.int32, (levels, BLOCK), 1)
    for block in range(blocks):
        inside = place < count_int - block * BLOCK
        vorticity = grid_part[pl.ds(block * fields, levels), :]
        spreading = grid_part[pl.ds(block * fields + levels, levels), :]
        thermal = grid_part[pl.ds(block * fields + 2 * levels, levels), :]
        lifting = -running_sum(thick * spreading)
        first = jnp.where(inside, -vorticity * spreading, 0.0)
        second = jnp.where(inside, 0.5 * (vorticity * vorticity - spreading * spreading), 0.0)
        third = jnp.where(inside, thermal * (factor * lifting - spreading), 0.0)
        tend[pl.ds(block * fields, levels), :] = first
        tend[pl.ds(block * fields + levels, levels), :] = second
        tend[pl.ds(block * fields + 2 * levels, levels), :] = third
        temp_ref[0, :, pl.ds(block * BLOCK, BLOCK)] = third.astype(jnp.bfloat16)

    left = tend[...].astype(jnp.bfloat16)
    scale = scale_ref[row]
    nt = (((1,), (1,)), ((), ()))
    for at in range(0, waves_all, 256):
        lanes = slice(at, at + 256)
        even = lax.dot_general(left, table_ref[0, 0, lanes, :], nt, preferred_element_type=jnp.float32)
        odd = lax.dot_general(left, table_ref[0, 1, lanes, :], nt, preferred_element_type=jnp.float32)
        real_sum = jnp.zeros((fields, 256), jnp.float32)
        imag_sum = jnp.zeros((fields, 256), jnp.float32)
        for block in range(blocks):
            cosine = phase_cos[block : block + 1, lanes]
            sine = phase_sin[block : block + 1, lanes]
            rows = slice(block * fields, (block + 1) * fields)
            real_sum += cosine * even[rows] + sine * odd[rows]
            imag_sum += cosine * odd[rows] - sine * even[rows]
        keep = jnp.where(kept[:, lanes], scale, 0.0)
        back_ref[0, :fields, lanes] = (real_sum * keep).astype(jnp.bfloat16)
        back_ref[0, fields:, lanes] = (imag_sum * keep).astype(jnp.bfloat16)


def row_trips(fourier, tables, waves, points, scales, thickness):
    rows, columns, waves_all = fourier.shape
    levels = thickness.shape[0]
    pressure = jnp.cumsum(thickness) - 0.5 * thickness
    stacked = PBUF // BLOCK * columns // 2
    whole = lambda i: (0, 0)
    return pl.pallas_call(
        row_kernel,
        grid=(rows,),
        out_shape=(
            jax.ShapeDtypeStruct((rows, columns, waves_all), jnp.bfloat16),
            jax.ShapeDtypeStruct((rows, levels, PBUF), jnp.bfloat16),
        ),
        in_specs=[
            pl.BlockSpec(memory_space=pltpu.SMEM),
            pl.BlockSpec(memory_space=pltpu.SMEM),
            pl.BlockSpec((1, waves_all), whole),
            pl.BlockSpec((levels, 1), whole),
            pl.BlockSpec((levels, 1), whole),
            pl.BlockSpec((1, columns, waves_all), lambda i: (i, 0, 0)),
            pl.BlockSpec((1, 2, waves_all, BLOCK), lambda i: (i, 0, 0, 0)),
        ],
        out_specs=(
            pl.BlockSpec((1, columns, waves_all), lambda i: (i, 0, 0)),
            pl.BlockSpec((1, levels, PBUF), lambda i: (i, 0, 0)),
        ),
        scratch_shapes=[
            pltpu.VMEM((stacked, 2 * waves_all), jnp.float32),
            pltpu.VMEM((stacked, BLOCK), jnp.float32),
            pltpu.VMEM((stacked, BLOCK), jnp.float32),
        ],
        compiler_params=pltpu.CompilerParams(vmem_limit_bytes=56 * 1024 * 1024),
        cost_estimate=pl.CostEstimate(
            flops=rows * stacked * waves_all * 2 * BLOCK * 4,
            bytes_accessed=rows * waves_all * BLOCK * 4,
            transcendentals=0,
        ),
        name="rows",
    )(points, scales, waves[None, :], thickness[:, None], pressure[:, None], fourier, tables)


def on_device(spectral, legendre, wave_map, row_map, points, row_weight, thickness):
    wave_count = lax.axis_size("wave")
    level_count = lax.axis_size("lev")
    device_count = wave_count * level_count
    device_flat = lax.axis_index("wave") * level_count + lax.axis_index("lev")
    slots_here = legendre.shape[0]
    waves_all = wave_map.shape[0]
    rows_all = row_map.shape[0]
    rows_here = rows_all // device_count
    levels = thickness.shape[0]
    columns = 6 * levels
    arrival_waves = (
        wave_map.reshape(wave_count, level_count, slots_here).transpose(1, 0, 2).reshape(-1)
    )
    owned_rows = lax.dynamic_slice_in_dim(row_map, device_flat * rows_here, rows_here)
    owned_points = jnp.take(points, owned_rows)
    owned_scales = jnp.take(row_weight, owned_rows) / owned_points.astype(jnp.float32)
    tables = make_tables(owned_points, arrival_waves)

    slot_coefs = lax.all_to_all(spectral, "lev", split_axis=0, concat_axis=3, tiled=True)
    local_waves = lax.dynamic_slice_in_dim(wave_map, device_flat * slots_here, slots_here)
    kept_mask = jnp.arange(waves_all, dtype=jnp.int32)[None, :] < (waves_all - local_waves)[:, None]
    masked_coefs = jnp.where(
        kept_mask[:, None, None, None, :], slot_coefs, jnp.zeros((), jnp.bfloat16)
    )
    fourier = jnp.einsum(
        "sfplk,skr->sfplr", masked_coefs, legendre, preferred_element_type=jnp.float32
    ).astype(jnp.bfloat16)
    fourier = fourier.transpose(0, 2, 1, 3, 4).reshape(slots_here, columns, rows_all)
    outgoing = jnp.take(fourier, row_map, axis=2)
    arrived = lax.all_to_all(
        lax.all_to_all(outgoing, "wave", split_axis=2, concat_axis=0, tiled=True),
        "lev",
        split_axis=2,
        concat_axis=0,
        tiled=True,
    )
    by_row = arrived.transpose(2, 1, 0)
    row_backs, row_temps = row_trips(
        by_row, tables, arrival_waves, owned_points, owned_scales, thickness
    )
    returning = row_backs.transpose(2, 1, 0)
    partial_back = lax.all_to_all(returning, "lev", split_axis=0, concat_axis=2, tiled=True)
    gathered = lax.all_to_all(partial_back, "wave", split_axis=0, concat_axis=2, tiled=True)
    positions = (
        jnp.zeros((rows_all,), jnp.int32).at[row_map].set(jnp.arange(rows_all, dtype=jnp.int32))
    )
    by_latitude = jnp.take(gathered, positions, axis=2)
    direct_sums = jnp.einsum(
        "scr,skr->sck", by_latitude, legendre, preferred_element_type=jnp.float32
    )
    spec_local = (
        jnp.where(kept_mask[:, None, :], direct_sums, 0.0)
        .astype(jnp.bfloat16)
        .reshape(slots_here, 2, 3, levels, waves_all)
        .transpose(0, 2, 1, 3, 4)
    )
    spec_tend = lax.all_to_all(spec_local, "lev", split_axis=3, concat_axis=0, tiled=True)
    return (spec_tend, row_temps)


def solution(mesh):
    return jax.shard_map(
        on_device,
        mesh=mesh,
        in_specs=(
            P("wave", None, None, "lev", None),
            P(("wave", "lev"), None, None),
            P(),
            P(),
            P(),
            P(),
            P(),
        ),
        out_specs=(P("wave", None, None, "lev", None), P(("wave", "lev"), None, None)),
        check_vma=False,
    )
```

```python
import jax
import jax.numpy as jnp
import numpy as np
from jax import lax
from jax.experimental import pallas as pl
from jax.experimental.pallas import tpu as pltpu
from jax.sharding import PartitionSpec as P

PBUF = 5376
BLOCK = 768
LANES = 128
MESH = pl.DeviceIdType.MESH
NT = (((1,), (1,)), ((), ()))
TN = (((0,), (0,)), ((), ()))
MIB = 1024 * 1024

adiabatic_exponent = 2.0 / 7.0

cos_terms = (0.9999999857, -19.73920338, 64.9390589, -85.44903786, 60.15837722, -25.93212729, 6.478082977)
sin_terms = (6.283185301, -41.34169993, 81.60510632, -76.70254382, 42.02196627, -14.88466424, 3.21649078)


def turn_cos_sin(turns):
    square = turns * turns
    cosine = jnp.full_like(turns, cos_terms[-1])
    for term in cos_terms[-2::-1]:
        cosine = cosine * square + term
    sine = jnp.full_like(turns, sin_terms[-1])
    for term in sin_terms[-2::-1]:
        sine = sine * square + term
    return cosine, sine * turns


def turns_of(product, count, inverse):
    return (product - count * jnp.round(product * inverse)) * inverse


def table_kernel(points_ref, waves_ref, table_ref):
    row = pl.program_id(0)
    count = points_ref[row].astype(jnp.float32)
    inverse = 1.0 / jnp.full((1, 1), count, jnp.float32)
    waves_all = waves_ref.shape[0]
    chunk = 64

    def one_chunk(index, carry):
        at = pl.multiple_of(index * chunk, chunk)
        waves = waves_ref[pl.ds(at, chunk), :]
        lane = lax.broadcasted_iota(jnp.int32, (chunk, LANES), 1).astype(jnp.float32)
        cosine, sine = turn_cos_sin(turns_of(waves * lane, count, inverse))
        step_cos, step_sin = turn_cos_sin(turns_of(waves * float(LANES), count, inverse))
        for piece in range(BLOCK // LANES):
            where = pl.ds(piece * LANES, LANES)
            table_ref[0, 0, pl.ds(at, chunk), where] = cosine.astype(jnp.bfloat16)
            table_ref[0, 1, pl.ds(at, chunk), where] = (-sine).astype(jnp.bfloat16)
            if piece + 1 < BLOCK // LANES:
                cosine, sine = (
                    cosine * step_cos - sine * step_sin,
                    sine * step_cos + cosine * step_sin,
                )
        return carry

    lax.fori_loop(0, waves_all // chunk, one_chunk, 0)


def make_tables(points, waves):
    rows, waves_all = points.shape[0], waves.shape[0]
    spread = jnp.broadcast_to(waves.astype(jnp.float32)[:, None], (waves_all, LANES))
    return pl.pallas_call(
        table_kernel,
        grid=(rows,),
        out_shape=jax.ShapeDtypeStruct((rows, 2, waves_all, BLOCK), jnp.bfloat16),
        in_specs=[
            pl.BlockSpec(memory_space=pltpu.SMEM),
            pl.BlockSpec((waves_all, LANES), lambda i: (0, 0)),
        ],
        out_specs=pl.BlockSpec((1, 2, waves_all, BLOCK), lambda i: (i, 0, 0, 0)),
        compiler_params=pltpu.CompilerParams(vmem_limit_bytes=40 * 1024 * 1024),
        cost_estimate=pl.CostEstimate(
            flops=rows * waves_all * BLOCK * 40,
            bytes_accessed=rows * waves_all * BLOCK * 4,
            transcendentals=0,
        ),
        name="tables",
    )(points, spread)


def running_sum(values):
    place = lax.broadcasted_iota(jnp.int32, (8, values.shape[1]), 0)
    before = jnp.zeros((1, values.shape[1]), jnp.float32)
    groups = []
    for start in range(0, values.shape[0], 8):
        part = values[start : start + 8]
        for shift in (1, 2, 4):
            part = part + jnp.where(place >= shift, pltpu.roll(part, shift, 0), 0.0)
        part = part + before
        before = part[7:8]
        groups.append(part)
    return jnp.concatenate(groups, axis=0)


def meet(axis_count, peer_of):
    barrier = pltpu.get_barrier_semaphore()

    def tell(step, carry):
        pl.semaphore_signal(barrier, inc=1, device_id=peer_of(step), device_id_type=MESH)
        return carry

    lax.fori_loop(1, axis_count, tell, 0)
    return barrier


def lev_peer(step):
    level = lax.axis_index("lev")
    return lax.axis_index("wave"), lax.rem(level + step, lax.axis_size("lev"))


def row_choice(rows_ref):
    rows_all = rows_ref.shape[1]
    return jnp.where(
        lax.broadcasted_iota(jnp.int32, (rows_all, rows_all), 0) == rows_ref[...], 1.0, 0.0
    ).astype(jnp.bfloat16)


def spread_kernel(
    waves_ref, rows_ref, spec_ref, legendre_ref, out_ref,
    recv, table, choice, stage, own_sem, table_sem, send_sem, recv_sem, send2_sem, recv2_sem,
):
    slots, groups = recv.shape[0], recv.shape[1]
    waves_all = recv.shape[-1]
    wave, level = lax.axis_index("wave"), lax.axis_index("lev")
    loads = [
        pltpu.make_async_copy(legendre_ref.at[s], table.at[s], table_sem.at[s]) for s in range(slots)
    ]
    own = [
        pltpu.make_async_copy(spec_ref.at[level * slots + s], recv.at[s, level], own_sem.at[s])
        for s in range(slots)
    ]
    barrier = meet(groups, lev_peer)
    own[0].start()
    loads[0].start()
    choice[...] = row_choice(rows_ref)
    pl.semaphore_wait(barrier, groups - 1)

    first, second = {}, {}
    for s in range(slots):
        for step in range(1, groups):
            peer = lax.rem(level + step, groups)
            first[s, step] = pltpu.make_async_remote_copy(
                src_ref=spec_ref.at[peer * slots + s],
                dst_ref=recv.at[s, level],
                send_sem=send_sem.at[s, step - 1],
                recv_sem=recv_sem.at[s, step - 1],
                device_id=(wave, peer),
                device_id_type=MESH,
            )
            first[s, step].start()
    for s in range(1, slots):
        own[s].start()
        loads[s].start()

    position = lax.broadcasted_iota(jnp.int32, (1, waves_all), 1)
    for s in range(slots):
        own[s].wait()
        for step in range(1, groups):
            first[s, step].wait_recv()
        loads[s].wait()
        coefs = recv[s].reshape(-1, waves_all)
        keep = jnp.where(position < waves_all - waves_ref[s], 1.0, 0.0)
        coefs = coefs * jnp.broadcast_to(keep, coefs.shape).astype(jnp.bfloat16)
        fourier = jnp.dot(coefs, table[s], preferred_element_type=jnp.float32).astype(jnp.bfloat16)
        placed = jnp.dot(fourier, choice[...], preferred_element_type=jnp.float32).astype(jnp.bfloat16)
        for group in range(groups):
            stage[s, group] = placed[:, group * LANES : (group + 1) * LANES]
        for step in range(1, groups):
            peer = lax.rem(level + step, groups)
            second[s, step] = pltpu.make_async_remote_copy(
                src_ref=stage.at[s, peer],
                dst_ref=out_ref.at[level, s],
                send_sem=send2_sem.at[s, step - 1],
                recv_sem=recv2_sem.at[s, step - 1],
                device_id=(wave, peer),
                device_id_type=MESH,
            )
            second[s, step].start()
        out_ref[level, s] = stage[s, level]
    for copy in list(first.values()) + list(second.values()):
        copy.wait_send()
    for copy in second.values():
        copy.wait_recv()


def spread(spec, legendre, local_waves, placed_rows):
    slots, waves_all, rows_all = legendre.shape
    groups = spec.shape[0] // slots
    pairs = spec.shape[1]
    columns = groups * pairs * 2
    dma = pltpu.SemaphoreType.DMA
    return pl.pallas_call(
        spread_kernel,
        out_shape=jax.ShapeDtypeStruct((groups, slots, columns, LANES), jnp.bfloat16),
        in_specs=[
            pl.BlockSpec(memory_space=pltpu.SMEM),
            pl.BlockSpec(memory_space=pltpu.VMEM),
            pl.BlockSpec(memory_space=pl.ANY),
            pl.BlockSpec(memory_space=pl.ANY),
        ],
        out_specs=pl.BlockSpec(memory_space=pltpu.VMEM),
        scratch_shapes=[
            pltpu.VMEM((slots, groups, pairs, 2, waves_all), jnp.bfloat16),
            pltpu.VMEM((slots, waves_all, rows_all), jnp.bfloat16),
            pltpu.VMEM((rows_all, rows_all), jnp.bfloat16),
            pltpu.VMEM((slots, groups, columns, LANES), jnp.bfloat16),
            dma((slots,)),
            dma((slots,)),
            dma((slots, groups - 1)),
            dma((slots, groups - 1)),
            dma((slots, groups - 1)),
            dma((slots, groups - 1)),
        ],
        compiler_params=pltpu.CompilerParams(
            collective_id=1, has_side_effects=True, vmem_limit_bytes=48 * MIB
        ),
        cost_estimate=pl.CostEstimate(
            flops=2 * slots * columns * rows_all * (waves_all + rows_all),
            bytes_accessed=slots * waves_all * rows_all * 2,
            transcendentals=0,
        ),
        name="spread",
    )(local_waves, placed_rows, spec, legendre)


def gather_kernel(
    waves_ref, rows_ref, x_ref, legendre_ref, out_ref,
    recv, table, choice, stage, table_sem, own_sem, send_sem, recv_sem, send2_sem, recv2_sem,
):
    groups, slots, columns, _ = recv.shape
    waves_all = table.shape[1]
    wave, level = lax.axis_index("wave"), lax.axis_index("lev")
    loads = [
        pltpu.make_async_copy(legendre_ref.at[s], table.at[s], table_sem.at[s]) for s in range(slots)
    ]
    barrier = meet(groups, lev_peer)
    loads[0].start()
    recv[level] = x_ref[level]
    choice[...] = row_choice(rows_ref)
    pl.semaphore_wait(barrier, groups - 1)

    first, second, own = {}, {}, {}
    for s in range(slots):
        for step in range(1, groups):
            peer = lax.rem(level + step, groups)
            first[s, step] = pltpu.make_async_remote_copy(
                src_ref=x_ref.at[peer, s],
                dst_ref=recv.at[level, s],
                send_sem=send_sem.at[s, step - 1],
                recv_sem=recv_sem.at[s, step - 1],
                device_id=(wave, peer),
                device_id_type=MESH,
            )
            first[s, step].start()
    for s in range(1, slots):
        loads[s].start()

    position = lax.broadcasted_iota(jnp.int32, (1, waves_all), 1)
    for s in range(slots):
        for step in range(1, groups):
            first[s, step].wait_recv()
        loads[s].wait()
        placed = jnp.concatenate([recv[group, s] for group in range(groups)], axis=1)
        back = lax.dot_general(placed, choice[...], NT, preferred_element_type=jnp.float32)
        sums = lax.dot_general(
            back.astype(jnp.bfloat16), table[s], NT, preferred_element_type=jnp.float32
        )
        sums = jnp.where(position < waves_all - waves_ref[s], sums, 0.0).astype(jnp.bfloat16)
        stage[s] = sums.reshape(stage.shape[1:])
        for step in range(1, groups):
            peer = lax.rem(level + step, groups)
            second[s, step] = pltpu.make_async_remote_copy(
                src_ref=stage.at[s, peer],
                dst_ref=out_ref.at[level * slots + s],
                send_sem=send2_sem.at[s, step - 1],
                recv_sem=recv2_sem.at[s, step - 1],
                device_id=(wave, peer),
                device_id_type=MESH,
            )
            second[s, step].start()
        own[s] = pltpu.make_async_copy(
            stage.at[s, level], out_ref.at[level * slots + s], own_sem.at[s]
        )
        own[s].start()
    for copy in list(first.values()) + list(second.values()):
        copy.wait_send()
    for copy in second.values():
        copy.wait_recv()
    for copy in own.values():
        copy.wait()


def gather(x, legendre, local_waves, placed_rows):
    slots, waves_all, rows_all = legendre.shape
    groups, _, columns, _ = x.shape
    pairs = columns // groups // 2
    dma = pltpu.SemaphoreType.DMA
    return pl.pallas_call(
        gather_kernel,
        out_shape=jax.ShapeDtypeStruct((groups * slots, pairs, 2, waves_all), jnp.bfloat16),
        in_specs=[
            pl.BlockSpec(memory_space=pltpu.SMEM),
            pl.BlockSpec(memory_space=pltpu.VMEM),
            pl.BlockSpec(memory_space=pltpu.VMEM),
            pl.BlockSpec(memory_space=pl.ANY),
        ],
        out_specs=pl.BlockSpec(memory_space=pl.ANY),
        scratch_shapes=[
            pltpu.VMEM((groups, slots, columns, LANES), jnp.bfloat16),
            pltpu.VMEM((slots, waves_all, rows_all), jnp.bfloat16),
            pltpu.VMEM((rows_all, rows_all), jnp.bfloat16),
            pltpu.VMEM((slots, groups, pairs, 2, waves_all), jnp.bfloat16),
            dma((slots,)),
            dma((slots,)),
            dma((slots, groups - 1)),
            dma((slots, groups - 1)),
            dma((slots, groups - 1)),
            dma((slots, groups - 1)),
        ],
        compiler_params=pltpu.CompilerParams(
            collective_id=2, has_side_effects=True, vmem_limit_bytes=48 * MIB
        ),
        cost_estimate=pl.CostEstimate(
            flops=2 * slots * columns * rows_all * (waves_all + rows_all),
            bytes_accessed=slots * waves_all * rows_all * 2,
            transcendentals=0,
        ),
        name="gather",
    )(local_waves, placed_rows, x, legendre)


def wave_peer(step):
    wave = lax.axis_index("wave")
    core, z, x = lax.rem(wave, 2), lax.rem(lax.div(wave, 2), 8), lax.div(wave, 16)
    z = lax.rem(z + lax.rem(step, 8), 8)
    x = lax.rem(x + lax.rem(lax.div(step, 8), 4), 4)
    core = lax.rem(core + lax.div(step, 32), 2)
    return (x * 8 + z) * 2 + core, lax.axis_index("lev")


def exchange(barrier, src, dst, own_sem, send_sem, recv_sem):
    count = src.shape[0]
    me = lax.axis_index("wave")
    own = pltpu.make_async_copy(src.at[me], dst.at[me], own_sem)
    own.start()
    pl.semaphore_wait(barrier, count - 1)

    def send(step, carry):
        peer = wave_peer(step)
        pltpu.make_async_remote_copy(
            src_ref=src.at[peer[0]],
            dst_ref=dst.at[me],
            send_sem=send_sem,
            recv_sem=recv_sem,
            device_id=peer,
            device_id_type=MESH,
        ).start()
        return carry

    lax.fori_loop(1, count, send, 0)
    own.wait()
    sent = src.at[pl.ds(0, count - 1)]
    pltpu.make_async_copy(sent, sent, send_sem).wait()
    come = dst.at[pl.ds(0, count - 1)]
    pltpu.make_async_copy(come, come, recv_sem).wait()


def unit(size):
    rows = lax.broadcasted_iota(jnp.int32, (size, size), 0)
    return jnp.where(rows == lax.broadcasted_iota(jnp.int32, (size, size), 1), 1.0, 0.0).astype(jnp.bfloat16)


def scatter_rows_kernel(x_ref, out_ref, padded, wide, send, own_sem, send_sem, recv_sem):
    groups, slots, columns, _ = x_ref.shape
    waves, lines, _ = out_ref.shape
    barrier = meet(waves, wave_peer)
    used = slots * columns
    tiles = padded.shape[0] // LANES
    rows_here = LANES // waves
    padded[pl.ds(used, padded.shape[0] - used), :] = jnp.zeros((padded.shape[0] - used, LANES), jnp.bfloat16)
    identity = unit(LANES)
    for group in range(groups):
        padded[:used, :] = x_ref[group].reshape(used, LANES)
        turned = lax.dot_general(identity, padded[...], NT, preferred_element_type=jnp.float32)
        for i in range(rows_here):
            for tile in range(tiles):
                line = (group * rows_here + i) * tiles + tile
                wide[pl.ds(line, waves, stride=lines), :] = turned[
                    i * waves : (i + 1) * waves, tile * LANES : (tile + 1) * LANES
                ]
    send[...] = wide[...].reshape(waves, lines, LANES).astype(jnp.bfloat16)
    exchange(barrier, send, out_ref, own_sem, send_sem, recv_sem)


def scatter_rows(x, waves):
    groups, slots, columns, _ = x.shape
    tiles = pl.cdiv(slots * columns, LANES)
    lines = groups * LANES // waves * tiles
    dma = pltpu.SemaphoreType.DMA
    return pl.pallas_call(
        scatter_rows_kernel,
        out_shape=jax.ShapeDtypeStruct((waves, lines, LANES), jnp.bfloat16),
        in_specs=[pl.BlockSpec(memory_space=pltpu.VMEM)],
        out_specs=pl.BlockSpec(memory_space=pltpu.VMEM),
        scratch_shapes=[
            pltpu.VMEM((tiles * LANES, LANES), jnp.bfloat16),
            pltpu.VMEM((waves * lines, LANES), jnp.float32),
            pltpu.VMEM((waves, lines, LANES), jnp.bfloat16),
            dma,
            dma,
            dma,
        ],
        compiler_params=pltpu.CompilerParams(
            collective_id=3, has_side_effects=True, vmem_limit_bytes=32 * MIB
        ),
        name="scatter_rows",
    )(x)


def collect_rows_kernel(x_ref, out_ref, recv, wide, own_sem, send_sem, recv_sem):
    groups, slots, columns, _ = out_ref.shape
    waves, lines, _ = x_ref.shape
    barrier = meet(waves, wave_peer)
    exchange(barrier, x_ref, recv, own_sem, send_sem, recv_sem)
    used = slots * columns
    tiles = pl.cdiv(used, LANES)
    rows_here = LANES // waves
    wide[...] = recv[...].astype(jnp.float32).reshape(waves * lines, LANES)
    identity = unit(LANES)
    for group in range(groups):
        parts = []
        for i in range(rows_here):
            line = (group * rows_here + i) * tiles
            parts.append(
                jnp.concatenate(
                    [wide[pl.ds(line + tile, waves, stride=lines), :] for tile in range(tiles)], axis=1
                )
            )
        placed = jnp.concatenate(parts, axis=0).astype(jnp.bfloat16)
        turned = lax.dot_general(placed, identity, TN, preferred_element_type=jnp.float32)
        out_ref[group] = turned[:used].astype(jnp.bfloat16).reshape(slots, columns, LANES)


def collect_rows(x, groups, slots, columns):
    waves, lines, _ = x.shape
    dma = pltpu.SemaphoreType.DMA
    return pl.pallas_call(
        collect_rows_kernel,
        out_shape=jax.ShapeDtypeStruct((groups, slots, columns, LANES), jnp.bfloat16),
        in_specs=[pl.BlockSpec(memory_space=pltpu.VMEM)],
        out_specs=pl.BlockSpec(memory_space=pltpu.VMEM),
        scratch_shapes=[
            pltpu.VMEM((waves, lines, LANES), jnp.bfloat16),
            pltpu.VMEM((waves * lines, LANES), jnp.float32),
            dma,
            dma,
            dma,
        ],
        compiler_params=pltpu.CompilerParams(
            collective_id=4, has_side_effects=True, vmem_limit_bytes=32 * MIB
        ),
        name="collect_rows",
    )(x)


def column_order(slots, levels, groups):
    columns = 6 * levels
    inner = levels // groups
    slot, part, field, group, level = np.meshgrid(
        *(np.arange(n) for n in (slots, 2, 3, groups, inner)), indexing="ij"
    )
    lane = (slot * columns + ((group * 3 + field) * inner + level) * 2 + part).reshape(-1)
    width = pl.cdiv(slots * columns, LANES) * LANES
    return (lane[:, None] == np.arange(width)[None, :]).astype(jnp.bfloat16)


def row_kernel(
    points_ref, scale_ref, waves_ref, thick_ref, press_ref, order_ref, come_ref, table_ref,
    go_ref, temp_ref, wide, leave, backs, rotated, grid_part, tend,
):
    row = pl.program_id(0)
    count_int = points_ref[row]
    count = count_int.astype(jnp.float32)
    inverse = 1.0 / jnp.full((1, 1), count, jnp.float32)
    waves = waves_ref[...].astype(jnp.float32)
    waves_all = waves.shape[1]
    fields = 3 * thick_ref.shape[0]
    levels = fields // 3
    columns = 2 * fields
    senders, lines, _ = come_ref.shape
    groups = waves_all * columns // (order_ref.shape[0] * senders)
    slots = order_ref.shape[0] // columns
    tiles = order_ref.shape[1] // LANES
    span = groups * senders

    @pl.when(row == 0)
    def _():
        wide[...] = come_ref[...].astype(jnp.float32).reshape(senders * lines, LANES)

    def line_of(group, tile):
        return (group * pl.num_programs(0) + row) * tiles + tile

    placed = jnp.concatenate(
        [
            jnp.concatenate(
                [wide[pl.ds(line_of(group, tile), senders, stride=lines), :] for tile in range(tiles)], axis=1
            )
            for group in range(groups)
        ],
        axis=0,
    ).astype(jnp.bfloat16)
    fourier = jnp.concatenate(
        [
            lax.dot_general(
                order_ref[slot * columns : (slot + 1) * columns, :], placed, NT, preferred_element_type=jnp.float32
            )
            for slot in range(slots)
        ],
        axis=1,
    )
    blocks = PBUF // BLOCK
    kept = 2.0 * waves < count
    weight = jnp.where(kept, jnp.where(waves == 0.0, 1.0, 2.0), 0.0)
    values = fourier * weight
    real, imag = values[:fields], values[fields:]

    starts = lax.broadcasted_iota(jnp.int32, (8, waves_all), 0).astype(jnp.float32) * float(BLOCK)
    phase_cos, phase_sin = turn_cos_sin(turns_of(waves * starts, count, inverse))
    for block in range(blocks):
        cosine = phase_cos[block : block + 1]
        sine = phase_sin[block : block + 1]
        there = pl.ds(block * fields, fields)
        rotated[there, :waves_all] = real * cosine - imag * sine
        rotated[there, waves_all:] = real * sine + imag * cosine

    left = rotated[...].astype(jnp.bfloat16)
    for at in range(0, BLOCK, 256):
        right = table_ref[0, :, :, at : at + 256].reshape(2 * waves_all, 256)
        grid_part[:, at : at + 256] = jnp.dot(left, right, preferred_element_type=jnp.float32)

    thick = thick_ref[...]
    factor = adiabatic_exponent / press_ref[...]
    place = lax.broadcasted_iota(jnp.int32, (levels, BLOCK), 1)
    for block in range(blocks):
        inside = place < count_int - block * BLOCK
        vorticity = grid_part[pl.ds(block * fields, levels), :]
        spreading = grid_part[pl.ds(block * fields + levels, levels), :]
        thermal = grid_part[pl.ds(block * fields + 2 * levels, levels), :]
        lifting = -running_sum(thick * spreading)
        first = jnp.where(inside, -vorticity * spreading, 0.0)
        second = jnp.where(inside, 0.5 * (vorticity * vorticity - spreading * spreading), 0.0)
        third = jnp.where(inside, thermal * (factor * lifting - spreading), 0.0)
        tend[pl.ds(block * fields, levels), :] = first
        tend[pl.ds(block * fields + levels, levels), :] = second
        tend[pl.ds(block * fields + 2 * levels, levels), :] = third
        temp_ref[0, :, pl.ds(block * BLOCK, BLOCK)] = third.astype(jnp.bfloat16)

    left = tend[...].astype(jnp.bfloat16)
    scale = scale_ref[row]
    for at in range(0, waves_all, 256):
        lanes = slice(at, at + 256)
        even = lax.dot_general(left, table_ref[0, 0, lanes, :], NT, preferred_element_type=jnp.float32)
        odd = lax.dot_general(left, table_ref[0, 1, lanes, :], NT, preferred_element_type=jnp.float32)
        real_sum = jnp.zeros((fields, 256), jnp.float32)
        imag_sum = jnp.zeros((fields, 256), jnp.float32)
        for block in range(blocks):
            cosine = phase_cos[block : block + 1, lanes]
            sine = phase_sin[block : block + 1, lanes]
            rows = slice(block * fields, (block + 1) * fields)
            real_sum += cosine * even[rows] + sine * odd[rows]
            imag_sum += cosine * odd[rows] - sine * even[rows]
        keep = jnp.where(kept[:, lanes], scale, 0.0)
        there = at // 256 * columns
        backs[there : there + fields, :] = real_sum * keep
        backs[there + fields : there + columns, :] = imag_sum * keep

    leaving = lax.dot_general(
        backs[...].astype(jnp.bfloat16), order_ref[...], TN, preferred_element_type=jnp.float32
    )
    for group in range(groups):
        for tile in range(tiles):
            leave[pl.ds(line_of(group, tile), senders, stride=lines), :] = leaving[
                group * senders : (group + 1) * senders, tile * LANES : (tile + 1) * LANES
            ]

    @pl.when(row == pl.num_programs(0) - 1)
    def _():
        go_ref[...] = leave[...].reshape(senders, lines, LANES).astype(jnp.bfloat16)


def row_trips(come, tables, waves, points, scales, thickness, slots):
    senders, lines, _ = come.shape
    rows = points.shape[0]
    waves_all = waves.shape[0]
    levels = thickness.shape[0]
    columns = 6 * levels
    groups = waves_all // (slots * senders)
    pressure = jnp.cumsum(thickness) - 0.5 * thickness
    order = column_order(slots, levels, groups)
    stacked = PBUF // BLOCK * columns // 2
    whole = lambda i: (0, 0)
    return pl.pallas_call(
        row_kernel,
        grid=(rows,),
        out_shape=(
            jax.ShapeDtypeStruct(come.shape, jnp.bfloat16),
            jax.ShapeDtypeStruct((rows, levels, PBUF), jnp.bfloat16),
        ),
        in_specs=[
            pl.BlockSpec(memory_space=pltpu.SMEM),
            pl.BlockSpec(memory_space=pltpu.SMEM),
            pl.BlockSpec((1, waves_all), whole),
            pl.BlockSpec((levels, 1), whole),
            pl.BlockSpec((levels, 1), whole),
            pl.BlockSpec(order.shape, whole),
            pl.BlockSpec(come.shape, lambda i: (0, 0, 0)),
            pl.BlockSpec((1, 2, waves_all, BLOCK), lambda i: (i, 0, 0, 0)),
        ],
        out_specs=(
            pl.BlockSpec(come.shape, lambda i: (0, 0, 0)),
            pl.BlockSpec((1, levels, PBUF), lambda i: (i, 0, 0)),
        ),
        scratch_shapes=[
            pltpu.VMEM((senders * lines, LANES), jnp.float32),
            pltpu.VMEM((senders * lines, LANES), jnp.float32),
            pltpu.VMEM((slots * columns, groups * senders), jnp.float32),
            pltpu.VMEM((stacked, 2 * waves_all), jnp.float32),
            pltpu.VMEM((stacked, BLOCK), jnp.float32),
            pltpu.VMEM((stacked, BLOCK), jnp.float32),
        ],
        compiler_params=pltpu.CompilerParams(vmem_limit_bytes=56 * MIB),
        cost_estimate=pl.CostEstimate(
            flops=rows * stacked * waves_all * 2 * BLOCK * 4,
            bytes_accessed=rows * waves_all * BLOCK * 4,
            transcendentals=0,
        ),
        name="rows",
    )(points, scales, waves[None, :], thickness[:, None], pressure[:, None], jnp.asarray(order), come, tables)


def on_device(spectral, legendre, wave_map, row_map, points, row_weight, thickness):
    wave_count = lax.axis_size("wave")
    level_count = lax.axis_size("lev")
    device_count = wave_count * level_count
    device_flat = lax.axis_index("wave") * level_count + lax.axis_index("lev")
    slots_here, waves_all, rows_all = legendre.shape
    rows_here = rows_all // device_count
    levels = thickness.shape[0]
    columns = 6 * levels
    arrival_waves = (
        wave_map.reshape(wave_count, level_count, slots_here).transpose(2, 1, 0).reshape(-1)
    )
    placed_rows = (
        row_map.reshape(wave_count, level_count, rows_here).transpose(1, 2, 0).reshape(1, rows_all)
    )
    owned_rows = lax.dynamic_slice_in_dim(row_map, device_flat * rows_here, rows_here)
    owned_points = jnp.take(points, owned_rows)
    owned_scales = jnp.take(row_weight, owned_rows) / owned_points.astype(jnp.float32)
    local_waves = lax.dynamic_slice_in_dim(wave_map, device_flat * slots_here, slots_here)
    tables = make_tables(owned_points, arrival_waves)

    slots_group, _, _, level_here, _ = spectral.shape
    pairs = spectral.transpose(0, 1, 3, 2, 4).reshape(slots_group, 3 * level_here, 2, waves_all)
    placed = spread(pairs, legendre, local_waves, placed_rows)
    come = scatter_rows(placed, wave_count)
    go, row_temps = row_trips(
        come, tables, arrival_waves, owned_points, owned_scales, thickness, slots_here
    )
    placed = collect_rows(go, level_count, slots_here, columns)
    pairs = gather(placed, legendre, local_waves, placed_rows)
    spec_tend = pairs.reshape(slots_group, 3, level_here, 2, waves_all).transpose(0, 1, 3, 2, 4)
    return (spec_tend, row_temps)


def solution(mesh):
    return jax.shard_map(
        on_device,
        mesh=mesh,
        in_specs=(
            P("wave", None, None, "lev", None),
            P(("wave", "lev"), None, None),
            P(),
            P(),
            P(),
            P(),
            P(),
        ),
        out_specs=(P("wave", None, None, "lev", None), P(("wave", "lev"), None, None)),
        check_vma=False,
    )
```

```python
import jax
import jax.numpy as jnp
import numpy as np
from jax import lax
from jax.experimental import pallas as pl
from jax.experimental.pallas import tpu as pltpu
from jax.sharding import PartitionSpec as P

PBUF = 5376
BLOCK = 768
LANES = 128
MESH = pl.DeviceIdType.MESH
NT = (((1,), (1,)), ((), ()))
TN = (((0,), (0,)), ((), ()))
MIB = 1024 * 1024

adiabatic_exponent = 2.0 / 7.0

cos_terms = (0.9999999857, -19.73920338, 64.9390589, -85.44903786, 60.15837722, -25.93212729, 6.478082977)
sin_terms = (6.283185301, -41.34169993, 81.60510632, -76.70254382, 42.02196627, -14.88466424, 3.21649078)


def turn_cos_sin(turns):
    square = turns * turns
    cosine = jnp.full_like(turns, cos_terms[-1])
    for term in cos_terms[-2::-1]:
        cosine = cosine * square + term
    sine = jnp.full_like(turns, sin_terms[-1])
    for term in sin_terms[-2::-1]:
        sine = sine * square + term
    return cosine, sine * turns


def turns_of(product, count, inverse):
    return (product - count * jnp.round(product * inverse)) * inverse


def lev_peer(step):
    level = lax.axis_index("lev")
    return lax.axis_index("wave"), lax.rem(level + step, lax.axis_size("lev"))


def wave_peer(step):
    wave = lax.axis_index("wave")
    core, z, x = lax.rem(wave, 2), lax.rem(lax.div(wave, 2), 8), lax.div(wave, 16)
    z = lax.rem(z + lax.rem(step, 8), 8)
    x = lax.rem(x + lax.rem(lax.div(step, 8), 4), 4)
    core = lax.rem(core + lax.div(step, 32), 2)
    return (x * 8 + z) * 2 + core, lax.axis_index("lev")


def meet(group_count, peer_of, barrier):
    def tell(step, carry):
        pl.semaphore_signal(barrier, inc=1, device_id=peer_of(step), device_id_type=MESH)
        return carry

    lax.fori_loop(1, group_count, tell, 0)


def reorder(values, source):
    count = values.shape[1]
    line = lax.broadcasted_iota(jnp.int32, (16, count), 0)
    digits = jnp.where(line == 0, values // 32, jnp.where(line == 1, values % 32, 0))
    digits = digits.astype(jnp.float32).astype(jnp.bfloat16)
    parts = []
    for at in range(0, count, 256):
        place = lax.broadcasted_iota(jnp.int32, (count, 256), 0)
        choose = jnp.where(place == source[:, at : at + 256], 1.0, 0.0).astype(jnp.bfloat16)
        moved = jnp.dot(digits, choose, preferred_element_type=jnp.float32)
        parts.append(moved[0:1] * 32.0 + moved[1:2])
    return jnp.concatenate(parts, axis=1)


def row_choice(rows, source):
    count = rows.shape[1]
    place = lax.broadcasted_iota(jnp.int32, (count, count), 0).astype(jnp.float32)
    return jnp.where(place == reorder(rows, source), 1.0, 0.0).astype(jnp.bfloat16)


def fill_tables(trig, columns, points, first, last):
    chunk = 64
    lane = lax.broadcasted_iota(jnp.int32, (chunk, LANES), 1).astype(jnp.float32)
    counts = [jnp.full((chunk, LANES), count.astype(jnp.float32), jnp.float32) for count in points]

    def one_chunk(index, carry):
        at = pl.multiple_of(index * chunk, chunk)
        waves = columns[pl.ds(at, chunk), :]
        for row, count in enumerate(counts):
            inverse = 1.0 / count
            cosine, sine = turn_cos_sin(turns_of(waves * lane, count, inverse))
            step_cos, step_sin = turn_cos_sin(turns_of(waves * float(LANES), count, inverse))
            for piece in range(BLOCK // LANES):
                where = pl.ds(piece * LANES, LANES)
                trig[row, 0, pl.ds(at, chunk), where] = cosine.astype(jnp.bfloat16)
                trig[row, 1, pl.ds(at, chunk), where] = (-sine).astype(jnp.bfloat16)
                if piece + 1 < BLOCK // LANES:
                    cosine, sine = (
                        cosine * step_cos - sine * step_sin,
                        sine * step_cos + cosine * step_sin,
                    )
        return carry

    lax.fori_loop(first // chunk, last // chunk, one_chunk, 0)


def unit(size):
    rows = lax.broadcasted_iota(jnp.int32, (size, size), 0)
    return jnp.where(rows == lax.broadcasted_iota(jnp.int32, (size, size), 1), 1.0, 0.0).astype(jnp.bfloat16)


def send_waves(src, dst, send_sem, recv_sem):
    me = lax.axis_index("wave")

    def send(step, carry):
        peer = wave_peer(step)
        pltpu.make_async_remote_copy(
            src_ref=src.at[peer[0]],
            dst_ref=dst.at[me],
            send_sem=send_sem,
            recv_sem=recv_sem,
            device_id=peer,
            device_id_type=MESH,
        ).start()
        return carry

    lax.fori_loop(1, src.shape[0], send, 0)


def wait_waves(ref, sem):
    part = ref.at[pl.ds(0, ref.shape[0] - 1)]
    pltpu.make_async_copy(part, part, sem).wait()


def forward_kernel(
    waves_s, rows_s, points_s, waves_ref, rows_ref, wave_source_ref, row_source_ref, spec_ref, legendre_ref,
    come_ref, order_ref, tables_ref,
    recv, legend, choice, stage, arrived, flat, wide, send, columns, trig,
    own_sem, legend_sem, table_sem, send1, recv1, send2, recv2, send3, recv3, own3,
):
    slots, groups = recv.shape[0], recv.shape[1]
    waves_all = recv.shape[-1]
    senders, lines = come_ref.shape[1], come_ref.shape[2] * come_ref.shape[3]
    wave, level = lax.axis_index("wave"), lax.axis_index("lev")
    device = wave * groups + level
    rows_here = LANES // senders
    tiles = lines // rows_here
    loads = [
        pltpu.make_async_copy(legendre_ref.at[s], legend.at[s], legend_sem.at[s]) for s in range(slots)
    ]
    own = [
        pltpu.make_async_copy(spec_ref.at[level * slots + s], recv.at[s, level], own_sem.at[s])
        for s in range(slots)
    ]
    barrier = pltpu.get_barrier_semaphore()
    meet(groups, lev_peer, barrier)
    meet(senders, wave_peer, barrier)
    for s in range(slots):
        own[s].start()
        loads[s].start()
    pl.semaphore_wait(barrier, groups + senders - 2)

    first, second, own_wave = {}, {}, {}

    def send_coefs(s):
        for step in range(1, groups):
            peer = lax.rem(level + step, groups)
            first[s, step] = pltpu.make_async_remote_copy(
                src_ref=spec_ref.at[peer * slots + s],
                dst_ref=recv.at[s, level],
                send_sem=send1.at[s, step - 1],
                recv_sem=recv1.at[s, step - 1],
                device_id=(wave, peer),
                device_id_type=MESH,
            )
            first[s, step].start()

    send_coefs(0)
    send_coefs(1)
    choice[...] = row_choice(rows_ref[...], row_source_ref[...])
    order_ref[...] = reorder(waves_ref[...], wave_source_ref[...])
    square = lax.broadcasted_iota(jnp.int32, (LANES, LANES), 0) == lax.broadcasted_iota(
        jnp.int32, (LANES, LANES), 1
    )
    for at in range(0, waves_all, LANES):
        diagonal = jnp.where(square, order_ref[:, at : at + LANES], 0.0)
        columns[at : at + LANES, :] = jnp.broadcast_to(
            jnp.sum(diagonal, axis=1, keepdims=True), (LANES, LANES)
        )
    flat[pl.ds(groups * stage.shape[2], flat.shape[0] - groups * stage.shape[2]), :] = jnp.zeros(
        (flat.shape[0] - groups * stage.shape[2], LANES), jnp.bfloat16
    )
    points = [points_s[rows_s[device * rows_here + i]] for i in range(rows_here)]
    identity = unit(LANES)

    def send_rows(s):
        for step in range(1, groups):
            second[s, step].wait_recv()
        flat[: groups * stage.shape[2], :] = arrived[s].reshape(-1, LANES)
        turned = lax.dot_general(identity, flat[...], NT, preferred_element_type=jnp.float32)
        for i in range(rows_here):
            for tile in range(tiles):
                wide[pl.ds(i * tiles + tile, senders, stride=lines), :] = turned[
                    i * senders : (i + 1) * senders, tile * LANES : (tile + 1) * LANES
                ]
        send[s] = wide[...].astype(jnp.bfloat16).reshape(send.shape[1:])
        own_wave[s] = pltpu.make_async_copy(send.at[s, wave], come_ref.at[s, wave], own3.at[s])
        own_wave[s].start()
        send_waves(send.at[s], come_ref.at[s], send3.at[s], recv3.at[s])

    position = lax.broadcasted_iota(jnp.int32, (1, waves_all), 1)
    share = waves_all // slots
    for s in range(slots):
        fill_tables(trig, columns, points, s * share, (s + 1) * share)
        own[s].wait()
        for step in range(1, groups):
            first[s, step].wait_recv()
        loads[s].wait()
        coefs = recv[s].reshape(-1, waves_all)
        keep = jnp.where(position < waves_all - waves_s[device * slots + s], 1.0, 0.0)
        coefs = coefs * jnp.broadcast_to(keep, coefs.shape).astype(jnp.bfloat16)
        fourier = jnp.dot(coefs, legend[s], preferred_element_type=jnp.float32).astype(jnp.bfloat16)
        placed = jnp.dot(fourier, choice[...], preferred_element_type=jnp.float32).astype(jnp.bfloat16)
        for group in range(groups):
            stage[s, group] = placed[:, group * LANES : (group + 1) * LANES]
        for step in range(1, groups):
            peer = lax.rem(level + step, groups)
            second[s, step] = pltpu.make_async_remote_copy(
                src_ref=stage.at[s, peer],
                dst_ref=arrived.at[s, level],
                send_sem=send2.at[s, step - 1],
                recv_sem=recv2.at[s, step - 1],
                device_id=(wave, peer),
                device_id_type=MESH,
            )
            second[s, step].start()
        if s + 2 < slots:
            send_coefs(s + 2)
        arrived[s, level] = stage[s, level]
        if s >= 1:
            send_rows(s - 1)
    store = pltpu.make_async_copy(trig, tables_ref, table_sem)
    store.start()
    send_rows(slots - 1)
    for copy in list(first.values()) + list(second.values()):
        copy.wait_send()
    for s in range(slots):
        own_wave[s].wait()
        wait_waves(send.at[s], send3.at[s])
        wait_waves(come_ref.at[s], recv3.at[s])
    store.wait()


def wave_source(senders, groups, slots):
    places = np.arange(senders * groups * slots).reshape(senders, groups, slots)
    return places.transpose(1, 2, 0).reshape(1, -1).astype(np.int32)


def row_source(senders, groups, rows_here):
    places = np.arange(senders * groups * rows_here).reshape(senders, groups, rows_here)
    return places.transpose(1, 2, 0).reshape(1, -1).astype(np.int32)


def forward(pairs, legendre, wave_map, row_map, points, senders):
    slots, waves_all, rows_all = legendre.shape
    groups = pairs.shape[0] // slots
    columns = groups * pairs.shape[1] * 2
    rows_here = rows_all // (senders * groups)
    tiles = pl.cdiv(groups * columns, LANES)
    lines = rows_here * tiles
    come = (slots, senders, lines // 2, 2, LANES)
    tables = (rows_here, 2, waves_all, BLOCK)
    dma = pltpu.SemaphoreType.DMA
    smem = pl.BlockSpec(memory_space=pltpu.SMEM)
    vmem = pl.BlockSpec(memory_space=pltpu.VMEM)
    anywhere = pl.BlockSpec(memory_space=pl.ANY)
    return pl.pallas_call(
        forward_kernel,
        out_shape=(
            jax.ShapeDtypeStruct(come, jnp.bfloat16),
            jax.ShapeDtypeStruct((1, waves_all), jnp.float32),
            jax.ShapeDtypeStruct(tables, jnp.bfloat16),
        ),
        in_specs=[smem, smem, smem, vmem, vmem, vmem, vmem, anywhere, anywhere],
        out_specs=(vmem, vmem, anywhere),
        scratch_shapes=[
            pltpu.VMEM((slots, groups) + pairs.shape[1:], jnp.bfloat16),
            pltpu.VMEM(legendre.shape, jnp.bfloat16),
            pltpu.VMEM((rows_all, rows_all), jnp.bfloat16),
            pltpu.VMEM((slots, groups, columns, LANES), jnp.bfloat16),
            pltpu.VMEM((slots, groups, columns, LANES), jnp.bfloat16),
            pltpu.VMEM((tiles * LANES, LANES), jnp.bfloat16),
            pltpu.VMEM((senders * lines, LANES), jnp.float32),
            pltpu.VMEM(come, jnp.bfloat16),
            pltpu.VMEM((waves_all, LANES), jnp.float32),
            pltpu.VMEM(tables, jnp.bfloat16),
            dma((slots,)),
            dma((slots,)),
            dma,
            dma((slots, groups - 1)),
            dma((slots, groups - 1)),
            dma((slots, groups - 1)),
            dma((slots, groups - 1)),
            dma((slots,)),
            dma((slots,)),
            dma((slots,)),
        ],
        compiler_params=pltpu.CompilerParams(
            collective_id=1, has_side_effects=True, vmem_limit_bytes=56 * MIB
        ),
        name="forward",
    )(
        wave_map, row_map, points, wave_map[None, :], row_map[None, :],
        jnp.asarray(wave_source(senders, groups, slots)), jnp.asarray(row_source(senders, groups, rows_here)),
        pairs, legendre,
    )


def backward_kernel(
    waves_s, rows_ref, row_source_ref, go_ref, legendre_ref, out_ref,
    back, legend, choice, wide, turned, arrived, stage,
    own_sem, legend_sem, send1, recv1, send2, recv2, send3, recv3, own3,
):
    slots, groups, columns, _ = turned.shape
    senders, lines = go_ref.shape[1], go_ref.shape[2] * go_ref.shape[3]
    waves_all = legend.shape[1]
    wave, level = lax.axis_index("wave"), lax.axis_index("lev")
    device = wave * groups + level
    rows_here = LANES // senders
    tiles = lines // rows_here
    loads = [
        pltpu.make_async_copy(legendre_ref.at[s], legend.at[s], legend_sem.at[s]) for s in range(slots)
    ]
    own_wave = [
        pltpu.make_async_copy(go_ref.at[s, wave], back.at[s, wave], own3.at[s]) for s in range(slots)
    ]
    barrier = pltpu.get_barrier_semaphore()
    meet(groups, lev_peer, barrier)
    meet(senders, wave_peer, barrier)
    for s in range(slots):
        own_wave[s].start()
        loads[s].start()
    pl.semaphore_wait(barrier, groups + senders - 2)

    first, second, own = {}, {}, {}

    def send_rows(s):
        send_waves(go_ref.at[s], back.at[s], send3.at[s], recv3.at[s])

    send_rows(0)
    send_rows(1)
    choice[...] = row_choice(rows_ref[...], row_source_ref[...])
    identity = unit(LANES)
    position = lax.broadcasted_iota(jnp.int32, (1, waves_all), 1)

    def turn(s):
        own_wave[s].wait()
        wait_waves(back.at[s], recv3.at[s])
        wide[...] = back[s].reshape(senders * lines, LANES).astype(jnp.float32)
        placed = jnp.concatenate(
            [
                jnp.concatenate(
                    [wide[pl.ds(i * tiles + tile, senders, stride=lines), :] for tile in range(tiles)], axis=1
                )
                for i in range(rows_here)
            ],
            axis=0,
        ).astype(jnp.bfloat16)
        moved = lax.dot_general(placed, identity, TN, preferred_element_type=jnp.float32)
        turned[s] = moved[: groups * columns].astype(jnp.bfloat16).reshape(groups, columns, LANES)
        for step in range(1, groups):
            peer = lax.rem(level + step, groups)
            first[s, step] = pltpu.make_async_remote_copy(
                src_ref=turned.at[s, peer],
                dst_ref=arrived.at[s, level],
                send_sem=send1.at[s, step - 1],
                recv_sem=recv1.at[s, step - 1],
                device_id=(wave, peer),
                device_id_type=MESH,
            )
            first[s, step].start()
        arrived[s, level] = turned[s, level]

    def finish(s):
        for step in range(1, groups):
            first[s, step].wait_recv()
        loads[s].wait()
        placed = jnp.concatenate([arrived[s, group] for group in range(groups)], axis=1)
        fourier = lax.dot_general(placed, choice[...], NT, preferred_element_type=jnp.float32)
        sums = lax.dot_general(
            fourier.astype(jnp.bfloat16), legend[s], NT, preferred_element_type=jnp.float32
        )
        kept = position < waves_all - waves_s[device * slots + s]
        stage[s] = jnp.where(kept, sums, 0.0).astype(jnp.bfloat16).reshape(stage.shape[1:])
        for step in range(1, groups):
            peer = lax.rem(level + step, groups)
            second[s, step] = pltpu.make_async_remote_copy(
                src_ref=stage.at[s, peer],
                dst_ref=out_ref.at[level * slots + s],
                send_sem=send2.at[s, step - 1],
                recv_sem=recv2.at[s, step - 1],
                device_id=(wave, peer),
                device_id_type=MESH,
            )
            second[s, step].start()
        own[s] = pltpu.make_async_copy(stage.at[s, level], out_ref.at[level * slots + s], own_sem.at[s])
        own[s].start()

    for s in range(slots):
        turn(s)
        if s + 2 < slots:
            send_rows(s + 2)
        if s >= 1:
            finish(s - 1)
    finish(slots - 1)
    for s in range(slots):
        wait_waves(go_ref.at[s], send3.at[s])
        own[s].wait()
    for copy in list(first.values()) + list(second.values()):
        copy.wait_send()
    for copy in second.values():
        copy.wait_recv()


def backward(go, legendre, wave_map, row_map, groups, columns):
    slots, waves_all, rows_all = legendre.shape
    senders, lines = go.shape[1], go.shape[2] * 2
    rows_here = rows_all // (senders * groups)
    pairs = columns // groups // 2
    dma = pltpu.SemaphoreType.DMA
    smem = pl.BlockSpec(memory_space=pltpu.SMEM)
    vmem = pl.BlockSpec(memory_space=pltpu.VMEM)
    anywhere = pl.BlockSpec(memory_space=pl.ANY)
    return pl.pallas_call(
        backward_kernel,
        out_shape=jax.ShapeDtypeStruct((groups * slots, pairs, 2, waves_all), jnp.bfloat16),
        in_specs=[smem, vmem, vmem, vmem, anywhere],
        out_specs=anywhere,
        scratch_shapes=[
            pltpu.VMEM(go.shape, jnp.bfloat16),
            pltpu.VMEM(legendre.shape, jnp.bfloat16),
            pltpu.VMEM((rows_all, rows_all), jnp.bfloat16),
            pltpu.VMEM((senders * lines, LANES), jnp.float32),
            pltpu.VMEM((slots, groups, columns, LANES), jnp.bfloat16),
            pltpu.VMEM((slots, groups, columns, LANES), jnp.bfloat16),
            pltpu.VMEM((slots, groups, pairs, 2, waves_all), jnp.bfloat16),
            dma((slots,)),
            dma((slots,)),
            dma((slots, groups - 1)),
            dma((slots, groups - 1)),
            dma((slots, groups - 1)),
            dma((slots, groups - 1)),
            dma((slots,)),
            dma((slots,)),
            dma((slots,)),
        ],
        compiler_params=pltpu.CompilerParams(
            collective_id=2, has_side_effects=True, vmem_limit_bytes=56 * MIB
        ),
        name="backward",
    )(wave_map, row_map[None, :], jnp.asarray(row_source(senders, groups, rows_here)), go, legendre)


def running_sum(values):
    place = lax.broadcasted_iota(jnp.int32, (8, values.shape[1]), 0)
    before = jnp.zeros((1, values.shape[1]), jnp.float32)
    groups = []
    for start in range(0, values.shape[0], 8):
        part = values[start : start + 8]
        for shift in (1, 2, 4):
            part = part + jnp.where(place >= shift, pltpu.roll(part, shift, 0), 0.0)
        part = part + before
        before = part[7:8]
        groups.append(part)
    return jnp.concatenate(groups, axis=0)


def row_kernel(
    rows_s, points_s, weight_s, waves_ref, thick_ref, order_ref, come_ref, table_ref,
    go_ref, temp_ref, wide, leave, backs, rotated, grid_part, tend,
):
    row = pl.program_id(0)
    slots, senders = come_ref.shape[0], come_ref.shape[1]
    lines = come_ref.shape[2] * come_ref.shape[3]
    waves = waves_ref[...]
    waves_all = waves.shape[1]
    groups = waves_all // (slots * senders)
    span = slots * senders
    levels = thick_ref.shape[1]
    fields, columns = 3 * levels, 6 * levels
    tiles = order_ref.shape[1] // LANES
    device = lax.axis_index("wave") * lax.axis_size("lev") + lax.axis_index("lev")
    grid_row = rows_s[device * pl.num_programs(0) + row]
    count_int = points_s[grid_row]
    count = count_int.astype(jnp.float32)
    inverse = 1.0 / jnp.full((1, 1), count, jnp.float32)
    scale = weight_s[grid_row] * inverse
    blocks = PBUF // BLOCK

    @pl.when(row == 0)
    def _():
        wide[...] = come_ref[...].reshape(slots * senders * lines, LANES).astype(jnp.float32)

    def line_of(slot, tile):
        return slot * (senders * lines) + row * tiles + tile

    placed = jnp.concatenate(
        [
            jnp.concatenate(
                [wide[pl.ds(line_of(slot, tile), senders, stride=lines), :] for tile in range(tiles)], axis=1
            )
            for slot in range(slots)
        ],
        axis=0,
    ).astype(jnp.bfloat16)
    ordered = lax.dot_general(order_ref[...], placed, NT, preferred_element_type=jnp.float32)
    fourier = jnp.concatenate(
        [ordered[group * columns : (group + 1) * columns] for group in range(groups)], axis=1
    )
    kept = 2.0 * waves < count
    weight = jnp.where(kept, jnp.where(waves == 0.0, 1.0, 2.0), 0.0)
    values = fourier * weight
    real, imag = values[:fields], values[fields:]

    starts = lax.broadcasted_iota(jnp.int32, (8, waves_all), 0).astype(jnp.float32) * float(BLOCK)
    phase_cos, phase_sin = turn_cos_sin(turns_of(waves * starts, count, inverse))
    for at in range(0, waves_all, 256):
        lanes = slice(at, at + 256)
        here_real, here_imag = real[:, lanes], imag[:, lanes]
        parts = [], []
        for block in range(blocks):
            cosine = phase_cos[block : block + 1, lanes]
            sine = phase_sin[block : block + 1, lanes]
            parts[0].append(here_real * cosine - here_imag * sine)
            parts[1].append(here_real * sine + here_imag * cosine)
        rotated[:, lanes] = jnp.concatenate(parts[0], axis=0).astype(jnp.bfloat16)
        rotated[:, at + waves_all : at + waves_all + 256] = jnp.concatenate(parts[1], axis=0).astype(jnp.bfloat16)

    for at in range(0, BLOCK, 256):
        right = table_ref[0, :, :, at : at + 256].reshape(2 * waves_all, 256)
        grid_part[:, at : at + 256] = jnp.dot(rotated[...], right, preferred_element_type=jnp.float32)

    above = lax.broadcasted_iota(jnp.int32, (levels, levels), 0) - lax.broadcasted_iota(
        jnp.int32, (levels, levels), 1
    )
    thick_line = jnp.broadcast_to(thick_ref[...], (levels, levels))
    thick = jnp.sum(jnp.where(above == 0, thick_line, 0.0), axis=1, keepdims=True)
    pressure = jnp.sum(jnp.where(above >= 0, thick_line, 0.0), axis=1, keepdims=True) - 0.5 * thick
    factor = adiabatic_exponent / pressure
    place = lax.broadcasted_iota(jnp.int32, (levels, BLOCK), 1)
    for block in range(blocks):
        inside = place < count_int - block * BLOCK
        vorticity = grid_part[pl.ds(block * fields, levels), :]
        spreading = grid_part[pl.ds(block * fields + levels, levels), :]
        thermal = grid_part[pl.ds(block * fields + 2 * levels, levels), :]
        lifting = -running_sum(thick * spreading)
        first = jnp.where(inside, -vorticity * spreading, 0.0)
        second = jnp.where(inside, 0.5 * (vorticity * vorticity - spreading * spreading), 0.0)
        third = jnp.where(inside, thermal * (factor * lifting - spreading), 0.0)
        tend[pl.ds(block * fields, levels), :] = first
        tend[pl.ds(block * fields + levels, levels), :] = second
        tend[pl.ds(block * fields + 2 * levels, levels), :] = third
        temp_ref[0, :, pl.ds(block * BLOCK, BLOCK)] = third.astype(jnp.bfloat16)

    left = tend[...].astype(jnp.bfloat16)
    for at in range(0, waves_all, 256):
        lanes = slice(at, at + 256)
        even = lax.dot_general(left, table_ref[0, 0, lanes, :], NT, preferred_element_type=jnp.float32)
        odd = lax.dot_general(left, table_ref[0, 1, lanes, :], NT, preferred_element_type=jnp.float32)
        real_sum = jnp.zeros((fields, 256), jnp.float32)
        imag_sum = jnp.zeros((fields, 256), jnp.float32)
        for block in range(blocks):
            cosine = phase_cos[block : block + 1, lanes]
            sine = phase_sin[block : block + 1, lanes]
            rows = slice(block * fields, (block + 1) * fields)
            real_sum += cosine * even[rows] + sine * odd[rows]
            imag_sum += cosine * odd[rows] - sine * even[rows]
        keep = jnp.where(kept[:, lanes], scale, 0.0)
        backs[:fields, lanes] = real_sum * keep
        backs[fields:, lanes] = imag_sum * keep

    stacked = jnp.concatenate(
        [backs[:, group * span : (group + 1) * span] for group in range(groups)], axis=0
    ).astype(jnp.bfloat16)
    leaving = lax.dot_general(stacked, order_ref[...], TN, preferred_element_type=jnp.float32)
    for slot in range(slots):
        for tile in range(tiles):
            leave[pl.ds(line_of(slot, tile), senders, stride=lines), :] = leaving[
                slot * senders : (slot + 1) * senders, tile * LANES : (tile + 1) * LANES
            ]

    @pl.when(row == pl.num_programs(0) - 1)
    def _():
        go_ref[...] = leave[...].astype(jnp.bfloat16).reshape(go_ref.shape)


def column_order(levels, groups):
    columns = 6 * levels
    inner = levels // groups
    sender, part, field, group, level = np.meshgrid(
        *(np.arange(n) for n in (groups, 2, 3, groups, inner)), indexing="ij"
    )
    lane = (sender * columns + ((group * 3 + field) * inner + level) * 2 + part).reshape(-1)
    width = pl.cdiv(groups * columns, LANES) * LANES
    return (lane[:, None] == np.arange(width)[None, :]).astype(jnp.bfloat16)


def row_trips(come, tables, waves, row_map, points, row_weight, thickness, groups):
    rows, _, waves_all, _ = tables.shape
    levels = thickness.shape[0]
    columns = 6 * levels
    order = column_order(levels, groups)
    stacked = PBUF // BLOCK * columns // 2
    whole = lambda i: (0, 0)
    whole_come = lambda i: (0,) * come.ndim
    smem = pl.BlockSpec(memory_space=pltpu.SMEM)
    return pl.pallas_call(
        row_kernel,
        grid=(rows,),
        out_shape=(
            jax.ShapeDtypeStruct(come.shape, jnp.bfloat16),
            jax.ShapeDtypeStruct((rows, levels, PBUF), jnp.bfloat16),
        ),
        in_specs=[
            smem,
            smem,
            smem,
            pl.BlockSpec((1, waves_all), whole),
            pl.BlockSpec((1, levels), whole),
            pl.BlockSpec(order.shape, whole),
            pl.BlockSpec(come.shape, whole_come),
            pl.BlockSpec((1, 2, waves_all, BLOCK), lambda i: (i, 0, 0, 0)),
        ],
        out_specs=(
            pl.BlockSpec(come.shape, whole_come),
            pl.BlockSpec((1, levels, PBUF), lambda i: (i, 0, 0)),
        ),
        scratch_shapes=[
            pltpu.VMEM((come.size // LANES, LANES), jnp.float32),
            pltpu.VMEM((come.size // LANES, LANES), jnp.float32),
            pltpu.VMEM((columns, waves_all), jnp.float32),
            pltpu.VMEM((stacked, 2 * waves_all), jnp.bfloat16),
            pltpu.VMEM((stacked, BLOCK), jnp.float32),
            pltpu.VMEM((stacked, BLOCK), jnp.float32),
        ],
        compiler_params=pltpu.CompilerParams(vmem_limit_bytes=56 * MIB),
        cost_estimate=pl.CostEstimate(
            flops=rows * stacked * waves_all * 2 * BLOCK * 4,
            bytes_accessed=rows * waves_all * BLOCK * 4,
            transcendentals=0,
        ),
        name="rows",
    )(row_map, points, row_weight, waves, thickness[None, :], jnp.asarray(order), come, tables)


def on_device(spectral, legendre, wave_map, row_map, points, row_weight, thickness):
    senders, groups = lax.axis_size("wave"), lax.axis_size("lev")
    slots_group, fields, _, levels_here, waves_all = spectral.shape
    columns = 2 * fields * thickness.shape[0]
    pairs = spectral.transpose(0, 1, 3, 2, 4).reshape(slots_group, fields * levels_here, 2, waves_all)
    come, waves, tables = forward(pairs, legendre, wave_map, row_map, points, senders)
    go, row_temps = row_trips(come, tables, waves, row_map, points, row_weight, thickness, groups)
    pairs = backward(go, legendre, wave_map, row_map, groups, columns)
    spec_tend = pairs.reshape(slots_group, fields, levels_here, 2, waves_all).transpose(0, 1, 3, 2, 4)
    return (spec_tend, row_temps)


def solution(mesh):
    return jax.shard_map(
        on_device,
        mesh=mesh,
        in_specs=(
            P("wave", None, None, "lev", None),
            P(("wave", "lev"), None, None),
            P(),
            P(),
            P(),
            P(),
            P(),
        ),
        out_specs=(P("wave", None, None, "lev", None), P(("wave", "lev"), None, None)),
        check_vma=False,
    )
```

```python
import jax
import jax.numpy as jnp
import numpy as np
from jax import lax
from jax.experimental import pallas as pl
from jax.experimental.pallas import tpu as pltpu
from jax.sharding import PartitionSpec as P

PBUF = 5376
BLOCK = 768
LANES = 128
MESH = pl.DeviceIdType.MESH
NT = (((1,), (1,)), ((), ()))
TN = (((0,), (0,)), ((), ()))
MIB = 1024 * 1024

adiabatic_exponent = 2.0 / 7.0

cos_terms = (0.9999999857, -19.73920338, 64.9390589, -85.44903786, 60.15837722, -25.93212729, 6.478082977)
sin_terms = (6.283185301, -41.34169993, 81.60510632, -76.70254382, 42.02196627, -14.88466424, 3.21649078)


def turn_cos_sin(turns):
    square = turns * turns
    cosine = jnp.full_like(turns, cos_terms[-1])
    for term in cos_terms[-2::-1]:
        cosine = cosine * square + term
    sine = jnp.full_like(turns, sin_terms[-1])
    for term in sin_terms[-2::-1]:
        sine = sine * square + term
    return cosine, sine * turns


def turns_of(product, count, inverse):
    return (product - count * jnp.round(product * inverse)) * inverse


def lev_peer(step):
    level = lax.axis_index("lev")
    return lax.axis_index("wave"), lax.rem(level + step, lax.axis_size("lev"))


ALONG_X, ALONG_Z, CORES = 4, 8, 2
HUBS = ALONG_X * CORES


def hub_and_z():
    wave = lax.axis_index("wave")
    return lax.div(wave, ALONG_Z * CORES) * CORES + lax.rem(wave, CORES), lax.rem(lax.div(wave, CORES), ALONG_Z)


def device_at(hub, z):
    return (lax.div(hub, CORES) * ALONG_Z + z) * CORES + lax.rem(hub, CORES), lax.axis_index("lev")


def hub_peer(step):
    hub, z = hub_and_z()
    return device_at(lax.rem(hub + step, HUBS), z)


def z_peer(step):
    hub, z = hub_and_z()
    return device_at(hub, lax.rem(z + step, ALONG_Z))


def meet(group_count, peer_of, barrier):
    def tell(step, carry):
        pl.semaphore_signal(barrier, inc=1, device_id=peer_of(step), device_id_type=MESH)
        return carry

    lax.fori_loop(1, group_count, tell, 0)


def reorder(values, source):
    count = values.shape[1]
    line = lax.broadcasted_iota(jnp.int32, (16, count), 0)
    digits = jnp.where(line == 0, values // 32, jnp.where(line == 1, values % 32, 0))
    digits = digits.astype(jnp.float32).astype(jnp.bfloat16)
    parts = []
    for at in range(0, count, 256):
        place = lax.broadcasted_iota(jnp.int32, (count, 256), 0)
        choose = jnp.where(place == source[:, at : at + 256], 1.0, 0.0).astype(jnp.bfloat16)
        moved = jnp.dot(digits, choose, preferred_element_type=jnp.float32)
        parts.append(moved[0:1] * 32.0 + moved[1:2])
    return jnp.concatenate(parts, axis=1)


def row_choice(rows, source):
    count = rows.shape[1]
    place = lax.broadcasted_iota(jnp.int32, (count, count), 0).astype(jnp.float32)
    return jnp.where(place == reorder(rows, source), 1.0, 0.0).astype(jnp.bfloat16)


def fill_tables(trig, columns, points, first, last):
    chunk = 64
    lane = lax.broadcasted_iota(jnp.int32, (chunk, LANES), 1).astype(jnp.float32)
    counts = [jnp.full((chunk, LANES), count.astype(jnp.float32), jnp.float32) for count in points]

    def one_chunk(index, carry):
        at = pl.multiple_of(index * chunk, chunk)
        waves = columns[pl.ds(at, chunk), :]
        for row, count in enumerate(counts):
            inverse = 1.0 / count
            cosine, sine = turn_cos_sin(turns_of(waves * lane, count, inverse))
            step_cos, step_sin = turn_cos_sin(turns_of(waves * float(LANES), count, inverse))
            for piece in range(BLOCK // LANES):
                where = pl.ds(piece * LANES, LANES)
                trig[row, 0, pl.ds(at, chunk), where] = cosine.astype(jnp.bfloat16)
                trig[row, 1, pl.ds(at, chunk), where] = (-sine).astype(jnp.bfloat16)
                if piece + 1 < BLOCK // LANES:
                    cosine, sine = (
                        cosine * step_cos - sine * step_sin,
                        sine * step_cos + cosine * step_sin,
                    )
        return carry

    lax.fori_loop(first // chunk, last // chunk, one_chunk, 0)


def unit(size):
    rows = lax.broadcasted_iota(jnp.int32, (size, size), 0)
    return jnp.where(rows == lax.broadcasted_iota(jnp.int32, (size, size), 1), 1.0, 0.0).astype(jnp.bfloat16)


def wait_blocks(ref, sem):
    part = ref.at[pl.ds(0, ref.shape[0] - 1)]
    pltpu.make_async_copy(part, part, sem).wait()


def running_sum(values):
    place = lax.broadcasted_iota(jnp.int32, (8, values.shape[1]), 0)
    before = jnp.zeros((1, values.shape[1]), jnp.float32)
    groups = []
    for start in range(0, values.shape[0], 8):
        part = values[start : start + 8]
        for shift in (1, 2, 4):
            part = part + jnp.where(place >= shift, pltpu.roll(part, shift, 0), 0.0)
        part = part + before
        before = part[7:8]
        groups.append(part)
    return jnp.concatenate(groups, axis=0)


def trip_kernel(
    waves_s, rows_s, points_s, weight_s,
    waves_ref, rows_ref, wave_source_ref, row_source_ref, thick_ref, order_ref, spec_ref, legendre_ref,
    out_ref, temp_ref,
    recv, legend, choice, stage, arrived, flat, wide, send, come, columns, trig, waves_row, phases, grid_part, tend,
    middle, go, middle_back, back, turned, returned, result, order32, order,
    own_sem, legend_sem, order_sem, send1, recv1, send2, recv2, send3, recv3, own3,
    send4, recv4, own4, send5, recv5, send6, recv6, own6,
    send7, recv7, own7, send8, recv8, own8,
):
    slots, groups = recv.shape[0], recv.shape[1]
    waves_all = recv.shape[-1]
    senders, lines = come.shape[1] * come.shape[2], come.shape[3] * come.shape[4]
    hub, z = hub_and_z()
    cells = stage.shape[2]
    used = groups * cells
    wave, level = lax.axis_index("wave"), lax.axis_index("lev")
    device = wave * groups + level
    rows_here = LANES // senders
    tiles = lines // rows_here
    share = groups * senders
    levels = thick_ref.shape[1]
    fields = 3 * levels
    blocks = PBUF // BLOCK
    loads = [
        pltpu.make_async_copy(legendre_ref.at[s], legend.at[s], legend_sem.at[s]) for s in range(slots)
    ]
    own = [
        pltpu.make_async_copy(spec_ref.at[level * slots + s], recv.at[s, level], own_sem.at[s])
        for s in range(slots)
    ]
    barrier = pltpu.get_barrier_semaphore()
    meet(groups, lev_peer, barrier)
    meet(HUBS, hub_peer, barrier)
    meet(ALONG_Z, z_peer, barrier)
    for s in range(slots):
        own[s].start()
        loads[s].start()
    load_order = pltpu.make_async_copy(order_ref, order32, order_sem)
    load_order.start()
    choice[...] = row_choice(rows_ref[...], row_source_ref[...])
    pl.semaphore_wait(barrier, groups + HUBS + ALONG_Z - 3)

    def lev_copies(src_of, dst_of, send_sem, recv_sem, s):
        made = []
        for step in range(1, groups):
            peer = lax.rem(level + step, groups)
            made.append(
                pltpu.make_async_remote_copy(
                    src_ref=src_of(peer),
                    dst_ref=dst_of,
                    send_sem=send_sem.at[s, step - 1],
                    recv_sem=recv_sem.at[s, step - 1],
                    device_id=(wave, peer),
                    device_id_type=MESH,
                )
            )
            made[-1].start()
        return made

    coefs_out, rows_out, rows_back, tend_out = {}, {}, {}, {}
    own_middle, own_come, own_middle_back, own_back, own_out = {}, {}, {}, {}, {}

    def spread(src_of, dst, send_sem, recv_sem, own_sem, peer_of, me, count):
        own_block = pltpu.make_async_copy(src_of(me), dst.at[me], own_sem)
        own_block.start()

        def send_one(step, carry):
            pltpu.make_async_remote_copy(
                src_ref=src_of(lax.rem(me + step, count)),
                dst_ref=dst.at[me],
                send_sem=send_sem,
                recv_sem=recv_sem,
                device_id=peer_of(step),
                device_id_type=MESH,
            ).start()
            return carry

        lax.fori_loop(1, count, send_one, 0)
        return own_block

    def send_coefs(s):
        coefs_out[s] = lev_copies(lambda peer: spec_ref.at[peer * slots + s], recv.at[s, level], send1, recv1, s)

    send_coefs(0)
    send_coefs(1)
    waves_row[...] = reorder(
        jnp.concatenate([waves_ref[line : line + 1, :] for line in range(waves_ref.shape[0])], axis=1),
        wave_source_ref[...],
    )
    square = lax.broadcasted_iota(jnp.int32, (LANES, LANES), 0) == lax.broadcasted_iota(
        jnp.int32, (LANES, LANES), 1
    )
    for at in range(0, waves_all, LANES):
        diagonal = jnp.where(square, waves_row[:, at : at + LANES], 0.0)
        columns[at : at + LANES, :] = jnp.broadcast_to(
            jnp.sum(diagonal, axis=1, keepdims=True), (LANES, LANES)
        )
    load_order.wait()
    order[...] = order32[...].astype(jnp.bfloat16)
    flat[used:, :] = jnp.zeros((flat.shape[0] - used, LANES), jnp.bfloat16)
    identity = unit(LANES)
    position = lax.broadcasted_iota(jnp.int32, (1, waves_all), 1)
    grid_rows = [rows_s[device * rows_here + i] for i in range(rows_here)]
    points = [points_s[row] for row in grid_rows]
    counts = [jnp.full((1, 1), count.astype(jnp.float32), jnp.float32) for count in points]
    scales = [weight_s[row] / count for row, count in zip(grid_rows, counts)]
    starts = lax.broadcasted_iota(jnp.int32, (8, waves_all), 0).astype(jnp.float32) * float(BLOCK)
    for i in range(rows_here):
        phases[i, 0], phases[i, 1] = turn_cos_sin(turns_of(waves_row[...] * starts, counts[i], 1.0 / counts[i]))

    def kept_waves(i, s):
        return 2.0 * waves_row[:, s * share : (s + 1) * share] < counts[i]

    def transform(s):
        own[s].wait()
        for copy in coefs_out[s]:
            copy.wait_recv()
        loads[s].wait()
        coefs = recv[s].reshape(-1, waves_all)
        keep = jnp.where(position < waves_all - waves_s[device * slots + s], 1.0, 0.0)
        coefs = coefs * jnp.broadcast_to(keep, coefs.shape).astype(jnp.bfloat16)
        fourier = jnp.dot(coefs, legend[s], preferred_element_type=jnp.float32).astype(jnp.bfloat16)
        placed = jnp.dot(fourier, choice[...], preferred_element_type=jnp.float32).astype(jnp.bfloat16)
        for group in range(groups):
            stage[s, group] = placed[:, group * LANES : (group + 1) * LANES]
        rows_out[s] = lev_copies(lambda peer: stage.at[s, peer], arrived.at[s, level], send2, recv2, s)
        arrived[s, level] = stage[s, level]

    def send_rows(s):
        for copy in rows_out[s]:
            copy.wait_recv()
        flat[:used, :] = arrived[s].reshape(-1, LANES)
        moved = lax.dot_general(identity, flat[...], NT, preferred_element_type=jnp.float32)
        for i in range(rows_here):
            for tile in range(tiles):
                wide[pl.ds(i * tiles + tile, senders, stride=lines), :] = moved[
                    i * senders : (i + 1) * senders, tile * LANES : (tile + 1) * LANES
                ]
        send[s] = wide[...].astype(jnp.bfloat16).reshape(send.shape[1:])
        own_middle[s] = spread(
            lambda p: send.at[s, p], middle.at[s], send3.at[s], recv3.at[s], own3.at[s], z_peer, z, ALONG_Z
        )

    def hop(s):
        own_middle[s].wait()
        wait_blocks(middle.at[s], recv3.at[s])
        own_come[s] = spread(
            lambda p: middle.at[s, :, p], come.at[s], send7.at[s], recv7.at[s], own7.at[s], hub_peer, hub, HUBS
        )

    def read_lines(ref, s):
        wide[...] = ref[s].reshape(senders * lines, LANES).astype(jnp.float32)
        return jnp.concatenate(
            [
                jnp.concatenate(
                    [wide[pl.ds(i * tiles + tile, senders, stride=lines), :] for tile in range(tiles)], axis=1
                )
                for i in range(rows_here)
            ],
            axis=0,
        ).astype(jnp.bfloat16)

    def absorb(s):
        own_come[s].wait()
        wait_blocks(come.at[s], recv7.at[s])
        ordered = lax.dot_general(order[...], read_lines(come, s), NT, preferred_element_type=jnp.float32)
        lanes = slice(s * share, (s + 1) * share)
        waves = waves_row[:, lanes]
        for i in range(rows_here):
            fourier = jnp.concatenate(
                [
                    ordered[group * cells : (group + 1) * cells, i * senders : (i + 1) * senders]
                    for group in range(groups)
                ],
                axis=1,
            )
            fourier = fourier * jnp.where(kept_waves(i, s), jnp.where(waves == 0.0, 1.0, 2.0), 0.0)
            real, imag = fourier[:fields], fourier[fields:]
            parts = [], []
            for block in range(blocks):
                cosine = phases[i, 0, block : block + 1, lanes]
                sine = phases[i, 1, block : block + 1, lanes]
                parts[0].append(real * cosine - imag * sine)
                parts[1].append(real * sine + imag * cosine)
            left = jnp.concatenate(
                [jnp.concatenate(part, axis=0).astype(jnp.bfloat16) for part in parts], axis=1
            )
            for at in range(0, BLOCK, 256):
                right = trig[i, :, lanes, at : at + 256].reshape(2 * share, 256)
                added = jnp.dot(left, right, preferred_element_type=jnp.float32)
                if s == 0:
                    grid_part[i, :, at : at + 256] = added
                else:
                    grid_part[i, :, at : at + 256] += added

    def products(i):
        above = lax.broadcasted_iota(jnp.int32, (levels, levels), 0) - lax.broadcasted_iota(
            jnp.int32, (levels, levels), 1
        )
        thick_line = jnp.broadcast_to(thick_ref[...], (levels, levels))
        thick = jnp.sum(jnp.where(above == 0, thick_line, 0.0), axis=1, keepdims=True)
        pressure = jnp.sum(jnp.where(above >= 0, thick_line, 0.0), axis=1, keepdims=True) - 0.5 * thick
        factor = adiabatic_exponent / pressure
        place = lax.broadcasted_iota(jnp.int32, (levels, BLOCK), 1)
        parts = []
        for block in range(blocks):
            inside = place < points[i] - block * BLOCK
            at = block * fields
            vorticity = grid_part[i, at : at + levels, :]
            spreading = grid_part[i, at + levels : at + 2 * levels, :]
            thermal = grid_part[i, at + 2 * levels : at + 3 * levels, :]
            lifting = -running_sum(thick * spreading)
            first = jnp.where(inside, -vorticity * spreading, 0.0)
            second = jnp.where(inside, 0.5 * (vorticity * vorticity - spreading * spreading), 0.0)
            third = jnp.where(inside, thermal * (factor * lifting - spreading), 0.0)
            grid_part[i, at : at + levels, :] = first
            grid_part[i, at + levels : at + 2 * levels, :] = second
            grid_part[i, at + 2 * levels : at + 3 * levels, :] = third
            temp_ref[i, :, block * BLOCK : (block + 1) * BLOCK] = third.astype(jnp.bfloat16)
        tend[i] = grid_part[i].astype(jnp.bfloat16)

    def emit(s):
        lanes = slice(s * share, (s + 1) * share)
        pieces = []
        for i in range(rows_here):
            even = lax.dot_general(tend[i], trig[i, 0, lanes, :], NT, preferred_element_type=jnp.float32)
            odd = lax.dot_general(tend[i], trig[i, 1, lanes, :], NT, preferred_element_type=jnp.float32)
            real_sum = jnp.zeros((fields, share), jnp.float32)
            imag_sum = jnp.zeros((fields, share), jnp.float32)
            for block in range(blocks):
                cosine = phases[i, 0, block : block + 1, lanes]
                sine = phases[i, 1, block : block + 1, lanes]
                rows = slice(block * fields, (block + 1) * fields)
                real_sum += cosine * even[rows] + sine * odd[rows]
                imag_sum += cosine * odd[rows] - sine * even[rows]
            sums = jnp.concatenate([real_sum, imag_sum], axis=0) * jnp.where(kept_waves(i, s), scales[i], 0.0)
            pieces.append(
                jnp.concatenate(
                    [sums[:, group * senders : (group + 1) * senders] for group in range(groups)], axis=0
                )
            )
        stacked = jnp.concatenate(pieces, axis=1).astype(jnp.bfloat16)
        leaving = lax.dot_general(stacked, order[...], TN, preferred_element_type=jnp.float32)
        for i in range(rows_here):
            for tile in range(tiles):
                wide[pl.ds(i * tiles + tile, senders, stride=lines), :] = leaving[
                    i * senders : (i + 1) * senders, tile * LANES : (tile + 1) * LANES
                ]
        go[s] = wide[...].astype(jnp.bfloat16).reshape(go.shape[1:])
        own_middle_back[s] = spread(
            lambda p: go.at[s, p], middle_back.at[s], send4.at[s], recv4.at[s], own4.at[s], hub_peer, hub, HUBS
        )

    def hop_back(s):
        own_middle_back[s].wait()
        wait_blocks(middle_back.at[s], recv4.at[s])
        own_back[s] = spread(
            lambda p: middle_back.at[s, :, p], back.at[s], send8.at[s], recv8.at[s], own8.at[s], z_peer, z, ALONG_Z
        )

    def turn(s):
        own_back[s].wait()
        wait_blocks(back.at[s], recv8.at[s])
        moved = lax.dot_general(read_lines(back, s), identity, TN, preferred_element_type=jnp.float32)
        turned[s] = moved[:used].astype(jnp.bfloat16).reshape(groups, cells, LANES)
        rows_back[s] = lev_copies(lambda peer: turned.at[s, peer], returned.at[s, level], send5, recv5, s)
        returned[s, level] = turned[s, level]

    def finish(s):
        for copy in rows_back[s]:
            copy.wait_recv()
        placed = jnp.concatenate([returned[s, group] for group in range(groups)], axis=1)
        fourier = lax.dot_general(placed, choice[...], NT, preferred_element_type=jnp.float32)
        sums = lax.dot_general(
            fourier.astype(jnp.bfloat16), legend[s], NT, preferred_element_type=jnp.float32
        )
        kept = position < waves_all - waves_s[device * slots + s]
        result[s] = jnp.where(kept, sums, 0.0).astype(jnp.bfloat16).reshape(result.shape[1:])
        tend_out[s] = lev_copies(
            lambda peer: result.at[s, peer], out_ref.at[level * slots + s], send6, recv6, s
        )
        own_out[s] = pltpu.make_async_copy(result.at[s, level], out_ref.at[level * slots + s], own6.at[s])
        own_out[s].start()

    for s in range(slots):
        fill_tables(trig, columns, points, s * share, (s + 1) * share)
        transform(s)
        if s + 2 < slots:
            send_coefs(s + 2)
        if s >= 1:
            send_rows(s - 1)
        if s >= 2:
            hop(s - 2)
        if s >= 3:
            absorb(s - 3)
    send_rows(slots - 1)
    hop(slots - 2)
    absorb(slots - 3)
    hop(slots - 1)
    absorb(slots - 2)
    absorb(slots - 1)
    for i in range(rows_here):
        products(i)
    for s in range(slots + 3):
        if s < slots:
            emit(s)
        if 1 <= s <= slots:
            hop_back(s - 1)
        if 2 <= s <= slots + 1:
            turn(s - 2)
        if s >= 3:
            finish(s - 3)
    for s in range(slots):
        for copy in coefs_out[s] + rows_out[s] + rows_back[s] + tend_out[s]:
            copy.wait_send()
        wait_blocks(send.at[s], send3.at[s])
        wait_blocks(come.at[s], send7.at[s])
        wait_blocks(go.at[s], send4.at[s])
        wait_blocks(back.at[s], send8.at[s])
        for copy in tend_out[s]:
            copy.wait_recv()
        own_out[s].wait()


def wave_source(groups, slots):
    places = np.arange(ALONG_X * ALONG_Z * CORES * groups * slots)
    places = places.reshape(ALONG_X, ALONG_Z, CORES, groups, slots).transpose(4, 3, 0, 2, 1)
    return places.reshape(1, -1).astype(np.int32)


def row_source(groups, rows_here):
    places = np.arange(ALONG_X * ALONG_Z * CORES * groups * rows_here)
    places = places.reshape(ALONG_X, ALONG_Z, CORES, groups, rows_here).transpose(3, 4, 1, 0, 2)
    return places.reshape(1, -1).astype(np.int32)


def column_order(levels, groups):
    columns = 6 * levels
    inner = levels // groups
    sender, part, field, group, level = np.meshgrid(
        *(np.arange(n) for n in (groups, 2, 3, groups, inner)), indexing="ij"
    )
    lane = (sender * columns + ((group * 3 + field) * inner + level) * 2 + part).reshape(-1)
    width = pl.cdiv(groups * columns, LANES) * LANES
    return (lane[:, None] == np.arange(width)[None, :]).astype(np.float32)


def round_trip(pairs, legendre, wave_map, row_map, points, row_weight, thickness, senders):
    slots, waves_all, rows_all = legendre.shape
    groups = pairs.shape[0] // slots
    levels = thickness.shape[0]
    columns = 6 * levels
    rows_here = rows_all // (senders * groups)
    tiles = pl.cdiv(groups * columns, LANES)
    lines = rows_here * tiles
    stacked = PBUF // BLOCK * columns // 2
    by_z = (slots, ALONG_Z, HUBS, lines // 2, 2, LANES)
    by_hub = (slots, HUBS, ALONG_Z, lines // 2, 2, LANES)
    order = column_order(levels, groups)
    by_group = (slots, groups, columns, LANES)
    by_level = (slots, groups) + pairs.shape[1:]
    bf16, f32 = jnp.bfloat16, jnp.float32
    dma = pltpu.SemaphoreType.DMA
    lev_sem = dma((slots, groups - 1))
    slot_sem = dma((slots,))
    smem = pl.BlockSpec(memory_space=pltpu.SMEM)
    vmem = pl.BlockSpec(memory_space=pltpu.VMEM)
    anywhere = pl.BlockSpec(memory_space=pl.ANY)
    return pl.pallas_call(
        trip_kernel,
        out_shape=(
            jax.ShapeDtypeStruct(pairs.shape, bf16),
            jax.ShapeDtypeStruct((rows_here, levels, PBUF), bf16),
        ),
        in_specs=[smem] * 4 + [vmem] * 5 + [anywhere] * 3,
        out_specs=(anywhere, vmem),
        scratch_shapes=[
            pltpu.VMEM(by_level, bf16),
            pltpu.VMEM(legendre.shape, bf16),
            pltpu.VMEM((rows_all, rows_all), bf16),
            pltpu.VMEM(by_group, bf16),
            pltpu.VMEM(by_group, bf16),
            pltpu.VMEM((tiles * LANES, LANES), bf16),
            pltpu.VMEM((senders * lines, LANES), f32),
            pltpu.VMEM(by_z, bf16),
            pltpu.VMEM(by_hub, bf16),
            pltpu.VMEM((waves_all, LANES), f32),
            pltpu.VMEM((rows_here, 2, waves_all, BLOCK), bf16),
            pltpu.VMEM((1, waves_all), f32),
            pltpu.VMEM((rows_here, 2, 8, waves_all), f32),
            pltpu.VMEM((rows_here, stacked, BLOCK), f32),
            pltpu.VMEM((rows_here, stacked, BLOCK), bf16),
            pltpu.VMEM(by_z, bf16),
            pltpu.VMEM(by_hub, bf16),
            pltpu.VMEM(by_hub, bf16),
            pltpu.VMEM(by_z, bf16),
            pltpu.VMEM(by_group, bf16),
            pltpu.VMEM(by_group, bf16),
            pltpu.VMEM(by_level, bf16),
            pltpu.VMEM(order.shape, f32),
            pltpu.VMEM(order.shape, bf16),
            slot_sem, slot_sem, dma, lev_sem, lev_sem, lev_sem, lev_sem, slot_sem, slot_sem, slot_sem,
            slot_sem, slot_sem, slot_sem, lev_sem, lev_sem, lev_sem, lev_sem, slot_sem,
            slot_sem, slot_sem, slot_sem, slot_sem, slot_sem, slot_sem,
        ],
        compiler_params=pltpu.CompilerParams(
            collective_id=1, has_side_effects=True, vmem_limit_bytes=56 * MIB
        ),
        name="trip",
    )(
        wave_map, row_map, points, row_weight, wave_map.reshape(-1, LANES), row_map[None, :],
        jnp.asarray(wave_source(groups, slots)), jnp.asarray(row_source(groups, rows_here)),
        thickness[None, :], jnp.asarray(order), pairs, legendre,
    )


def settle_kernel(*refs):
    count = (len(refs) - 2) // 3
    sources, targets, held = refs[:count], refs[count : 2 * count], refs[2 * count : 3 * count]
    in_sems, out_sems = refs[-2:]
    blocks = [(which, block) for which in range(count) for block in range(sources[which].shape[0])]
    arriving, leaving = [], []
    for place, (which, block) in enumerate(blocks):
        arriving.append(
            pltpu.make_async_copy(sources[which].at[block], held[which].at[block], in_sems.at[place])
        )
        arriving[-1].start()
    for place, (which, block) in enumerate(blocks):
        arriving[place].wait()
        leaving.append(
            pltpu.make_async_copy(held[which].at[block], targets[which].at[block], out_sems.at[place])
        )
        leaving[-1].start()
    for copy in leaving:
        copy.wait()


def settle(*arrays):
    anywhere = pl.BlockSpec(memory_space=pl.ANY)
    return pl.pallas_call(
        settle_kernel,
        out_shape=tuple(jax.ShapeDtypeStruct(array.shape, array.dtype) for array in arrays),
        in_specs=[anywhere] * len(arrays),
        out_specs=(anywhere,) * len(arrays),
        scratch_shapes=[pltpu.VMEM(array.shape, array.dtype) for array in arrays]
        + [pltpu.SemaphoreType.DMA((sum(array.shape[0] for array in arrays),))] * 2,
        compiler_params=pltpu.CompilerParams(vmem_limit_bytes=56 * MIB),
        name="settle",
    )(*arrays)


def on_device(spectral, legendre, wave_map, row_map, points, row_weight, thickness):
    slots_group, fields, _, levels_here, waves_all = spectral.shape
    pairs = spectral.transpose(0, 1, 3, 2, 4).reshape(slots_group, fields * levels_here, 2, waves_all)
    pairs, row_temps = round_trip(
        pairs, legendre, wave_map, row_map, points, row_weight, thickness, lax.axis_size("wave")
    )
    pairs, row_temps = settle(pairs, row_temps)
    spec_tend = pairs.reshape(slots_group, fields, levels_here, 2, waves_all).transpose(0, 1, 3, 2, 4)
    return (spec_tend, row_temps)


def solution(mesh):
    return jax.shard_map(
        on_device,
        mesh=mesh,
        in_specs=(
            P("wave", None, None, "lev", None),
            P(("wave", "lev"), None, None),
            P(),
            P(),
            P(),
            P(),
            P(),
        ),
        out_specs=(P("wave", None, None, "lev", None), P(("wave", "lev"), None, None)),
        check_vma=False,
    )
```

```python
import jax
import jax.numpy as jnp
import numpy as np
from jax import lax
from jax.experimental import pallas as pl
from jax.experimental.pallas import tpu as pltpu
from jax.sharding import PartitionSpec as P

PBUF = 5376
BLOCK = 768
LANES = 128
MESH = pl.DeviceIdType.MESH
NT = (((1,), (1,)), ((), ()))
TN = (((0,), (0,)), ((), ()))
MIB = 1024 * 1024

adiabatic_exponent = 2.0 / 7.0

cos_terms = (0.9999999857, -19.73920338, 64.9390589, -85.44903786, 60.15837722, -25.93212729, 6.478082977)
sin_terms = (6.283185301, -41.34169993, 81.60510632, -76.70254382, 42.02196627, -14.88466424, 3.21649078)


def turn_cos_sin(turns):
    square = turns * turns
    cosine = jnp.full_like(turns, cos_terms[-1])
    for term in cos_terms[-2::-1]:
        cosine = cosine * square + term
    sine = jnp.full_like(turns, sin_terms[-1])
    for term in sin_terms[-2::-1]:
        sine = sine * square + term
    return cosine, sine * turns


def turns_of(product, count, inverse):
    return (product - count * jnp.round(product * inverse)) * inverse


def lev_peer(step):
    level = lax.axis_index("lev")
    return lax.axis_index("wave"), lax.rem(level + step, lax.axis_size("lev"))


ALONG_X, ALONG_Z, CORES = 4, 8, 2
HUBS = ALONG_X * CORES


def hub_and_z():
    wave = lax.axis_index("wave")
    return lax.div(wave, ALONG_Z * CORES) * CORES + lax.rem(wave, CORES), lax.rem(lax.div(wave, CORES), ALONG_Z)


def device_at(hub, z):
    return (lax.div(hub, CORES) * ALONG_Z + z) * CORES + lax.rem(hub, CORES), lax.axis_index("lev")


def hub_peer(step):
    hub, z = hub_and_z()
    return device_at(lax.rem(hub + step, HUBS), z)


def z_peer(step):
    hub, z = hub_and_z()
    return device_at(hub, lax.rem(z + step, ALONG_Z))


def meet(group_count, peer_of, barrier):
    def tell(step, carry):
        pl.semaphore_signal(barrier, inc=1, device_id=peer_of(step), device_id_type=MESH)
        return carry

    lax.fori_loop(1, group_count, tell, 0)


def reorder(values, source):
    count = values.shape[1]
    line = lax.broadcasted_iota(jnp.int32, (16, count), 0)
    digits = jnp.where(line == 0, values // 32, jnp.where(line == 1, values % 32, 0))
    digits = digits.astype(jnp.float32).astype(jnp.bfloat16)
    parts = []
    for at in range(0, count, 256):
        place = lax.broadcasted_iota(jnp.int32, (count, 256), 0)
        choose = jnp.where(place == source[:, at : at + 256], 1.0, 0.0).astype(jnp.bfloat16)
        moved = jnp.dot(digits, choose, preferred_element_type=jnp.float32)
        parts.append(moved[0:1] * 32.0 + moved[1:2])
    return jnp.concatenate(parts, axis=1)


def row_choice(rows, source):
    count = rows.shape[1]
    place = lax.broadcasted_iota(jnp.int32, (count, count), 0).astype(jnp.float32)
    return jnp.where(place == reorder(rows, source), 1.0, 0.0).astype(jnp.bfloat16)


def fill_tables(trig, columns, points, first, last):
    chunk = 64
    lane = lax.broadcasted_iota(jnp.int32, (chunk, LANES), 1).astype(jnp.float32)
    counts = [jnp.full((chunk, LANES), count.astype(jnp.float32), jnp.float32) for count in points]

    def one_chunk(index, carry):
        at = pl.multiple_of(index * chunk, chunk)
        waves = columns[pl.ds(at, chunk), :]
        for row, count in enumerate(counts):
            inverse = 1.0 / count
            cosine, sine = turn_cos_sin(turns_of(waves * lane, count, inverse))
            step_cos, step_sin = turn_cos_sin(turns_of(waves * float(LANES), count, inverse))
            for piece in range(BLOCK // LANES):
                where = pl.ds(piece * LANES, LANES)
                trig[row, 0, pl.ds(at, chunk), where] = cosine.astype(jnp.bfloat16)
                trig[row, 1, pl.ds(at, chunk), where] = (-sine).astype(jnp.bfloat16)
                if piece + 1 < BLOCK // LANES:
                    cosine, sine = (
                        cosine * step_cos - sine * step_sin,
                        sine * step_cos + cosine * step_sin,
                    )
        return carry

    lax.fori_loop(first // chunk, last // chunk, one_chunk, 0)


def unit(size):
    rows = lax.broadcasted_iota(jnp.int32, (size, size), 0)
    return jnp.where(rows == lax.broadcasted_iota(jnp.int32, (size, size), 1), 1.0, 0.0).astype(jnp.bfloat16)


def wait_blocks(ref, sem):
    part = ref.at[pl.ds(0, ref.shape[0] - 1)]
    pltpu.make_async_copy(part, part, sem).wait()


def running_sum(values):
    place = lax.broadcasted_iota(jnp.int32, (8, values.shape[1]), 0)
    before = jnp.zeros((1, values.shape[1]), jnp.float32)
    groups = []
    for start in range(0, values.shape[0], 8):
        part = values[start : start + 8]
        for shift in (1, 2, 4):
            part = part + jnp.where(place >= shift, pltpu.roll(part, shift, 0), 0.0)
        part = part + before
        before = part[7:8]
        groups.append(part)
    return jnp.concatenate(groups, axis=0)


def trip_kernel(
    waves_s, rows_s, points_s, weight_s,
    waves_ref, rows_ref, wave_source_ref, row_source_ref, thick_ref, order_ref, spec_ref, legendre_ref,
    out_ref, temp_out_ref,
    temp_ref, temp_sem, recv, legend, choice, stage, arrived, flat, wide, send, come, columns, trig, waves_row, phases, grid_part, tend,
    middle, go, middle_back, back, turned, returned, result, order32, order,
    own_sem, legend_sem, order_sem, send1, recv1, send2, recv2, send3, recv3, own3,
    send4, recv4, own4, send5, recv5, send6, recv6, own6,
    send7, recv7, own7, send8, recv8, own8,
):
    slots, groups = recv.shape[0], recv.shape[1]
    waves_all = recv.shape[-1]
    senders, lines = come.shape[1] * come.shape[2], come.shape[3] * come.shape[4]
    hub, z = hub_and_z()
    cells = stage.shape[2]
    used = groups * cells
    wave, level = lax.axis_index("wave"), lax.axis_index("lev")
    device = wave * groups + level
    rows_here = LANES // senders
    tiles = lines // rows_here
    share = groups * senders
    levels = thick_ref.shape[1]
    fields = 3 * levels
    blocks = PBUF // BLOCK
    loads = [
        pltpu.make_async_copy(legendre_ref.at[s], legend.at[s], legend_sem.at[s]) for s in range(slots)
    ]
    own = [
        pltpu.make_async_copy(spec_ref.at[level * slots + s], recv.at[s, level], own_sem.at[s])
        for s in range(slots)
    ]
    barrier = pltpu.get_barrier_semaphore()
    meet(groups, lev_peer, barrier)
    meet(HUBS, hub_peer, barrier)
    meet(ALONG_Z, z_peer, barrier)
    for s in range(slots):
        own[s].start()
        loads[s].start()
    load_order = pltpu.make_async_copy(order_ref, order32, order_sem)
    load_order.start()
    choice[...] = row_choice(rows_ref[...], row_source_ref[...])
    pl.semaphore_wait(barrier, groups + HUBS + ALONG_Z - 3)

    def lev_copies(src_of, dst_of, send_sem, recv_sem, s):
        made = []
        for step in range(1, groups):
            peer = lax.rem(level + step, groups)
            made.append(
                pltpu.make_async_remote_copy(
                    src_ref=src_of(peer),
                    dst_ref=dst_of,
                    send_sem=send_sem.at[s, step - 1],
                    recv_sem=recv_sem.at[s, step - 1],
                    device_id=(wave, peer),
                    device_id_type=MESH,
                )
            )
            made[-1].start()
        return made

    coefs_out, rows_out, rows_back, tend_out = {}, {}, {}, {}
    own_middle, own_come, own_middle_back, own_back, own_out = {}, {}, {}, {}, {}

    def spread(src_of, dst, send_sem, recv_sem, own_sem, peer_of, me, count):
        own_block = pltpu.make_async_copy(src_of(me), dst.at[me], own_sem)
        own_block.start()

        def send_one(step, carry):
            pltpu.make_async_remote_copy(
                src_ref=src_of(lax.rem(me + step, count)),
                dst_ref=dst.at[me],
                send_sem=send_sem,
                recv_sem=recv_sem,
                device_id=peer_of(step),
                device_id_type=MESH,
            ).start()
            return carry

        lax.fori_loop(1, count, send_one, 0)
        return own_block

    def send_coefs(s):
        coefs_out[s] = lev_copies(lambda peer: spec_ref.at[peer * slots + s], recv.at[s, level], send1, recv1, s)

    send_coefs(0)
    send_coefs(1)
    waves_row[...] = reorder(
        jnp.concatenate([waves_ref[line : line + 1, :] for line in range(waves_ref.shape[0])], axis=1),
        wave_source_ref[...],
    )
    square = lax.broadcasted_iota(jnp.int32, (LANES, LANES), 0) == lax.broadcasted_iota(
        jnp.int32, (LANES, LANES), 1
    )
    for at in range(0, waves_all, LANES):
        diagonal = jnp.where(square, waves_row[:, at : at + LANES], 0.0)
        columns[at : at + LANES, :] = jnp.broadcast_to(
            jnp.sum(diagonal, axis=1, keepdims=True), (LANES, LANES)
        )
    load_order.wait()
    order[...] = order32[...].astype(jnp.bfloat16)
    flat[used:, :] = jnp.zeros((flat.shape[0] - used, LANES), jnp.bfloat16)
    identity = unit(LANES)
    position = lax.broadcasted_iota(jnp.int32, (1, waves_all), 1)
    grid_rows = [rows_s[device * rows_here + i] for i in range(rows_here)]
    points = [points_s[row] for row in grid_rows]
    counts = [jnp.full((1, 1), count.astype(jnp.float32), jnp.float32) for count in points]
    scales = [weight_s[row] / count for row, count in zip(grid_rows, counts)]
    starts = lax.broadcasted_iota(jnp.int32, (8, waves_all), 0).astype(jnp.float32) * float(BLOCK)
    for i in range(rows_here):
        phases[i, 0], phases[i, 1] = turn_cos_sin(turns_of(waves_row[...] * starts, counts[i], 1.0 / counts[i]))

    def kept_waves(i, s):
        return 2.0 * waves_row[:, s * share : (s + 1) * share] < counts[i]

    def transform(s):
        own[s].wait()
        for copy in coefs_out[s]:
            copy.wait_recv()
        loads[s].wait()
        coefs = recv[s].reshape(-1, waves_all)
        keep = jnp.where(position < waves_all - waves_s[device * slots + s], 1.0, 0.0)
        coefs = coefs * jnp.broadcast_to(keep, coefs.shape).astype(jnp.bfloat16)
        fourier = jnp.dot(coefs, legend[s], preferred_element_type=jnp.float32).astype(jnp.bfloat16)
        placed = jnp.dot(fourier, choice[...], preferred_element_type=jnp.float32).astype(jnp.bfloat16)
        for group in range(groups):
            stage[s, group] = placed[:, group * LANES : (group + 1) * LANES]
        rows_out[s] = lev_copies(lambda peer: stage.at[s, peer], arrived.at[s, level], send2, recv2, s)
        arrived[s, level] = stage[s, level]

    def send_rows(s):
        for copy in rows_out[s]:
            copy.wait_recv()
        flat[:used, :] = arrived[s].reshape(-1, LANES)
        moved = lax.dot_general(identity, flat[...], NT, preferred_element_type=jnp.float32)
        for i in range(rows_here):
            for tile in range(tiles):
                wide[pl.ds(i * tiles + tile, senders, stride=lines), :] = moved[
                    i * senders : (i + 1) * senders, tile * LANES : (tile + 1) * LANES
                ]
        send[s] = wide[...].astype(jnp.bfloat16).reshape(send.shape[1:])
        own_middle[s] = spread(
            lambda p: send.at[s, p], middle.at[s], send3.at[s], recv3.at[s], own3.at[s], z_peer, z, ALONG_Z
        )

    def hop(s):
        own_middle[s].wait()
        wait_blocks(middle.at[s], recv3.at[s])
        own_come[s] = spread(
            lambda p: middle.at[s, :, p], come.at[s], send7.at[s], recv7.at[s], own7.at[s], hub_peer, hub, HUBS
        )

    def read_lines(ref, s):
        wide[...] = ref[s].reshape(senders * lines, LANES).astype(jnp.float32)
        return jnp.concatenate(
            [
                jnp.concatenate(
                    [wide[pl.ds(i * tiles + tile, senders, stride=lines), :] for tile in range(tiles)], axis=1
                )
                for i in range(rows_here)
            ],
            axis=0,
        ).astype(jnp.bfloat16)

    def absorb(s):
        own_come[s].wait()
        wait_blocks(come.at[s], recv7.at[s])
        ordered = lax.dot_general(order[...], read_lines(come, s), NT, preferred_element_type=jnp.float32)
        lanes = slice(s * share, (s + 1) * share)
        waves = waves_row[:, lanes]
        for i in range(rows_here):
            fourier = jnp.concatenate(
                [
                    ordered[group * cells : (group + 1) * cells, i * senders : (i + 1) * senders]
                    for group in range(groups)
                ],
                axis=1,
            )
            fourier = fourier * jnp.where(kept_waves(i, s), jnp.where(waves == 0.0, 1.0, 2.0), 0.0)
            real, imag = fourier[:fields], fourier[fields:]
            parts = [], []
            for block in range(blocks):
                cosine = phases[i, 0, block : block + 1, lanes]
                sine = phases[i, 1, block : block + 1, lanes]
                parts[0].append(real * cosine - imag * sine)
                parts[1].append(real * sine + imag * cosine)
            left = jnp.concatenate(
                [jnp.concatenate(part, axis=0).astype(jnp.bfloat16) for part in parts], axis=1
            )
            for at in range(0, BLOCK, 256):
                right = trig[i, :, lanes, at : at + 256].reshape(2 * share, 256)
                added = jnp.dot(left, right, preferred_element_type=jnp.float32)
                if s == 0:
                    grid_part[i, :, at : at + 256] = added
                else:
                    grid_part[i, :, at : at + 256] += added

    def products(i):
        above = lax.broadcasted_iota(jnp.int32, (levels, levels), 0) - lax.broadcasted_iota(
            jnp.int32, (levels, levels), 1
        )
        thick_line = jnp.broadcast_to(thick_ref[...], (levels, levels))
        thick = jnp.sum(jnp.where(above == 0, thick_line, 0.0), axis=1, keepdims=True)
        pressure = jnp.sum(jnp.where(above >= 0, thick_line, 0.0), axis=1, keepdims=True) - 0.5 * thick
        factor = adiabatic_exponent / pressure
        place = lax.broadcasted_iota(jnp.int32, (levels, BLOCK), 1)
        parts = []
        for block in range(blocks):
            inside = place < points[i] - block * BLOCK
            at = block * fields
            vorticity = grid_part[i, at : at + levels, :]
            spreading = grid_part[i, at + levels : at + 2 * levels, :]
            thermal = grid_part[i, at + 2 * levels : at + 3 * levels, :]
            lifting = -running_sum(thick * spreading)
            first = jnp.where(inside, -vorticity * spreading, 0.0)
            second = jnp.where(inside, 0.5 * (vorticity * vorticity - spreading * spreading), 0.0)
            third = jnp.where(inside, thermal * (factor * lifting - spreading), 0.0)
            grid_part[i, at : at + levels, :] = first
            grid_part[i, at + levels : at + 2 * levels, :] = second
            grid_part[i, at + 2 * levels : at + 3 * levels, :] = third
            temp_ref[i, :, block * BLOCK : (block + 1) * BLOCK] = third.astype(jnp.bfloat16)
        tend[i] = grid_part[i].astype(jnp.bfloat16)

    def emit(s):
        lanes = slice(s * share, (s + 1) * share)
        pieces = []
        for i in range(rows_here):
            even = lax.dot_general(tend[i], trig[i, 0, lanes, :], NT, preferred_element_type=jnp.float32)
            odd = lax.dot_general(tend[i], trig[i, 1, lanes, :], NT, preferred_element_type=jnp.float32)
            real_sum = jnp.zeros((fields, share), jnp.float32)
            imag_sum = jnp.zeros((fields, share), jnp.float32)
            for block in range(blocks):
                cosine = phases[i, 0, block : block + 1, lanes]
                sine = phases[i, 1, block : block + 1, lanes]
                rows = slice(block * fields, (block + 1) * fields)
                real_sum += cosine * even[rows] + sine * odd[rows]
                imag_sum += cosine * odd[rows] - sine * even[rows]
            sums = jnp.concatenate([real_sum, imag_sum], axis=0) * jnp.where(kept_waves(i, s), scales[i], 0.0)
            pieces.append(
                jnp.concatenate(
                    [sums[:, group * senders : (group + 1) * senders] for group in range(groups)], axis=0
                )
            )
        stacked = jnp.concatenate(pieces, axis=1).astype(jnp.bfloat16)
        leaving = lax.dot_general(stacked, order[...], TN, preferred_element_type=jnp.float32)
        for i in range(rows_here):
            for tile in range(tiles):
                wide[pl.ds(i * tiles + tile, senders, stride=lines), :] = leaving[
                    i * senders : (i + 1) * senders, tile * LANES : (tile + 1) * LANES
                ]
        go[s] = wide[...].astype(jnp.bfloat16).reshape(go.shape[1:])
        own_middle_back[s] = spread(
            lambda p: go.at[s, p], middle_back.at[s], send4.at[s], recv4.at[s], own4.at[s], hub_peer, hub, HUBS
        )

    def hop_back(s):
        own_middle_back[s].wait()
        wait_blocks(middle_back.at[s], recv4.at[s])
        own_back[s] = spread(
            lambda p: middle_back.at[s, :, p], back.at[s], send8.at[s], recv8.at[s], own8.at[s], z_peer, z, ALONG_Z
        )

    def turn(s):
        own_back[s].wait()
        wait_blocks(back.at[s], recv8.at[s])
        moved = lax.dot_general(read_lines(back, s), identity, TN, preferred_element_type=jnp.float32)
        turned[s] = moved[:used].astype(jnp.bfloat16).reshape(groups, cells, LANES)
        rows_back[s] = lev_copies(lambda peer: turned.at[s, peer], returned.at[s, level], send5, recv5, s)
        returned[s, level] = turned[s, level]

    def finish(s):
        for copy in rows_back[s]:
            copy.wait_recv()
        placed = jnp.concatenate([returned[s, group] for group in range(groups)], axis=1)
        fourier = lax.dot_general(placed, choice[...], NT, preferred_element_type=jnp.float32)
        sums = lax.dot_general(
            fourier.astype(jnp.bfloat16), legend[s], NT, preferred_element_type=jnp.float32
        )
        kept = position < waves_all - waves_s[device * slots + s]
        result[s] = jnp.where(kept, sums, 0.0).astype(jnp.bfloat16).reshape(result.shape[1:])
        tend_out[s] = lev_copies(
            lambda peer: result.at[s, peer], out_ref.at[level * slots + s], send6, recv6, s
        )
        own_out[s] = pltpu.make_async_copy(result.at[s, level], out_ref.at[level * slots + s], own6.at[s])
        own_out[s].start()

    for s in range(slots):
        fill_tables(trig, columns, points, s * share, (s + 1) * share)
        transform(s)
        if s + 2 < slots:
            send_coefs(s + 2)
        if s >= 1:
            send_rows(s - 1)
        if s >= 2:
            hop(s - 2)
        if s >= 3:
            absorb(s - 3)
    send_rows(slots - 1)
    hop(slots - 2)
    absorb(slots - 3)
    hop(slots - 1)
    absorb(slots - 2)
    absorb(slots - 1)
    for i in range(rows_here):
        products(i)
    store = pltpu.make_async_copy(temp_ref, temp_out_ref, temp_sem)
    store.start()
    for s in range(slots + 3):
        if s < slots:
            emit(s)
        if 1 <= s <= slots:
            hop_back(s - 1)
        if 2 <= s <= slots + 1:
            turn(s - 2)
        if s >= 3:
            finish(s - 3)
    for s in range(slots):
        for copy in coefs_out[s] + rows_out[s] + rows_back[s] + tend_out[s]:
            copy.wait_send()
        wait_blocks(send.at[s], send3.at[s])
        wait_blocks(come.at[s], send7.at[s])
        wait_blocks(go.at[s], send4.at[s])
        wait_blocks(back.at[s], send8.at[s])
        for copy in tend_out[s]:
            copy.wait_recv()
        own_out[s].wait()
    store.wait()


def wave_source(groups, slots):
    places = np.arange(ALONG_X * ALONG_Z * CORES * groups * slots)
    places = places.reshape(ALONG_X, ALONG_Z, CORES, groups, slots).transpose(4, 3, 0, 2, 1)
    return places.reshape(1, -1).astype(np.int32)


def row_source(groups, rows_here):
    places = np.arange(ALONG_X * ALONG_Z * CORES * groups * rows_here)
    places = places.reshape(ALONG_X, ALONG_Z, CORES, groups, rows_here).transpose(3, 4, 1, 0, 2)
    return places.reshape(1, -1).astype(np.int32)


def column_order(levels, groups):
    columns = 6 * levels
    inner = levels // groups
    sender, part, field, group, level = np.meshgrid(
        *(np.arange(n) for n in (groups, 2, 3, groups, inner)), indexing="ij"
    )
    lane = (sender * columns + ((group * 3 + field) * inner + level) * 2 + part).reshape(-1)
    width = pl.cdiv(groups * columns, LANES) * LANES
    return (lane[:, None] == np.arange(width)[None, :]).astype(np.float32)


def round_trip(pairs, legendre, wave_map, row_map, points, row_weight, thickness, senders):
    slots, waves_all, rows_all = legendre.shape
    groups = pairs.shape[0] // slots
    levels = thickness.shape[0]
    columns = 6 * levels
    rows_here = rows_all // (senders * groups)
    tiles = pl.cdiv(groups * columns, LANES)
    lines = rows_here * tiles
    stacked = PBUF // BLOCK * columns // 2
    by_z = (slots, ALONG_Z, HUBS, lines // 2, 2, LANES)
    by_hub = (slots, HUBS, ALONG_Z, lines // 2, 2, LANES)
    order = column_order(levels, groups)
    by_group = (slots, groups, columns, LANES)
    by_level = (slots, groups) + pairs.shape[1:]
    bf16, f32 = jnp.bfloat16, jnp.float32
    dma = pltpu.SemaphoreType.DMA
    lev_sem = dma((slots, groups - 1))
    slot_sem = dma((slots,))
    smem = pl.BlockSpec(memory_space=pltpu.SMEM)
    vmem = pl.BlockSpec(memory_space=pltpu.VMEM)
    anywhere = pl.BlockSpec(memory_space=pl.ANY)
    return pl.pallas_call(
        trip_kernel,
        out_shape=(
            jax.ShapeDtypeStruct(pairs.shape, bf16),
            jax.ShapeDtypeStruct((rows_here, levels, PBUF), bf16),
        ),
        in_specs=[smem] * 4 + [vmem] * 5 + [anywhere] * 3,
        out_specs=(anywhere, anywhere),
        scratch_shapes=[
            pltpu.VMEM((rows_here, levels, PBUF), bf16),
            dma,
            pltpu.VMEM(by_level, bf16),
            pltpu.VMEM(legendre.shape, bf16),
            pltpu.VMEM((rows_all, rows_all), bf16),
            pltpu.VMEM(by_group, bf16),
            pltpu.VMEM(by_group, bf16),
            pltpu.VMEM((tiles * LANES, LANES), bf16),
            pltpu.VMEM((senders * lines, LANES), f32),
            pltpu.VMEM(by_z, bf16),
            pltpu.VMEM(by_hub, bf16),
            pltpu.VMEM((waves_all, LANES), f32),
            pltpu.VMEM((rows_here, 2, waves_all, BLOCK), bf16),
            pltpu.VMEM((1, waves_all), f32),
            pltpu.VMEM((rows_here, 2, 8, waves_all), f32),
            pltpu.VMEM((rows_here, stacked, BLOCK), f32),
            pltpu.VMEM((rows_here, stacked, BLOCK), bf16),
            pltpu.VMEM(by_z, bf16),
            pltpu.VMEM(by_hub, bf16),
            pltpu.VMEM(by_hub, bf16),
            pltpu.VMEM(by_z, bf16),
            pltpu.VMEM(by_group, bf16),
            pltpu.VMEM(by_group, bf16),
            pltpu.VMEM(by_level, bf16),
            pltpu.VMEM(order.shape, f32),
            pltpu.VMEM(order.shape, bf16),
            slot_sem, slot_sem, dma, lev_sem, lev_sem, lev_sem, lev_sem, slot_sem, slot_sem, slot_sem,
            slot_sem, slot_sem, slot_sem, lev_sem, lev_sem, lev_sem, lev_sem, slot_sem,
            slot_sem, slot_sem, slot_sem, slot_sem, slot_sem, slot_sem,
        ],
        compiler_params=pltpu.CompilerParams(
            collective_id=1, has_side_effects=True, vmem_limit_bytes=56 * MIB
        ),
        name="trip",
    )(
        wave_map, row_map, points, row_weight, wave_map.reshape(-1, LANES), row_map[None, :],
        jnp.asarray(wave_source(groups, slots)), jnp.asarray(row_source(groups, rows_here)),
        thickness[None, :], jnp.asarray(order), pairs, legendre,
    )


def settle_kernel(*refs):
    count = (len(refs) - 2) // 3
    sources, targets, held = refs[:count], refs[count : 2 * count], refs[2 * count : 3 * count]
    in_sems, out_sems = refs[-2:]
    blocks = [(which, block) for which in range(count) for block in range(sources[which].shape[0])]
    arriving, leaving = [], []
    for place, (which, block) in enumerate(blocks):
        arriving.append(
            pltpu.make_async_copy(sources[which].at[block], held[which].at[block], in_sems.at[place])
        )
        arriving[-1].start()
    for place, (which, block) in enumerate(blocks):
        arriving[place].wait()
        leaving.append(
            pltpu.make_async_copy(held[which].at[block], targets[which].at[block], out_sems.at[place])
        )
        leaving[-1].start()
    for copy in leaving:
        copy.wait()


def settle(*arrays):
    anywhere = pl.BlockSpec(memory_space=pl.ANY)
    return pl.pallas_call(
        settle_kernel,
        out_shape=tuple(jax.ShapeDtypeStruct(array.shape, array.dtype) for array in arrays),
        in_specs=[anywhere] * len(arrays),
        out_specs=(anywhere,) * len(arrays),
        scratch_shapes=[pltpu.VMEM(array.shape, array.dtype) for array in arrays]
        + [pltpu.SemaphoreType.DMA((sum(array.shape[0] for array in arrays),))] * 2,
        compiler_params=pltpu.CompilerParams(vmem_limit_bytes=56 * MIB),
        name="settle",
    )(*arrays)


def on_device(spectral, legendre, wave_map, row_map, points, row_weight, thickness):
    slots_group, fields, _, levels_here, waves_all = spectral.shape
    pairs = spectral.transpose(0, 1, 3, 2, 4).reshape(slots_group, fields * levels_here, 2, waves_all)
    pairs, row_temps = round_trip(
        pairs, legendre, wave_map, row_map, points, row_weight, thickness, lax.axis_size("wave")
    )
    pairs, row_temps = settle(pairs, row_temps)
    spec_tend = pairs.reshape(slots_group, fields, levels_here, 2, waves_all).transpose(0, 1, 3, 2, 4)
    return (spec_tend, row_temps)


def solution(mesh):
    return jax.shard_map(
        on_device,
        mesh=mesh,
        in_specs=(
            P("wave", None, None, "lev", None),
            P(("wave", "lev"), None, None),
            P(),
            P(),
            P(),
            P(),
            P(),
        ),
        out_specs=(P("wave", None, None, "lev", None), P(("wave", "lev"), None, None)),
        check_vma=False,
    )
```
